512 devices in a mesh: req: 16 (over y, x), head: 4 (over z_lo), exp: 8 (over z_hi, core).
Axes of the slice: x: 4, y: 4, z: 16 (z_hi: 4, z_lo: 4; z = z_hi * 4 + z_lo), core: 2. Of those that a mesh axis runs over, the one named last changes fastest.
Arguments:
- moe_input: bfloat16 [768, 7168], P(('req', 'head'), 'exp'), may hold values from -6 to 6
- route_ids: int32 [768, 3], P(('req', 'head')), may hold values from 0 to 23, all different within a row; in each aligned block of 12 rows (0 to 11, 12 to 23, ...) at most 2 rows name the same one
- route_weight: float32 [768, 3], P(('req', 'head')), may hold values from 0.1 to 1
- w_up: bfloat16 [24, 2560, 7168], P('exp', ('req', 'head')), may hold values from -0.0625 to 0.0625
- w_down: bfloat16 [24, 2560, 7168], P('exp', None, ('req', 'head')), may hold values from -0.125 to 0.125
- queries: bfloat16 [512, 64, 256], P(('req', 'head', 'exp')), may hold values from -24 to 24
- keys: bfloat16 [512, 1024, 256], P(('req', 'head', 'exp')), may hold values from -6 to 6
- values: bfloat16 [512, 1024, 256], P(('req', 'head', 'exp')), may hold values from -6 to 6
Outputs:
- moe_output: bfloat16 [768, 7168], P(('req', 'head'), 'exp')
- context: bfloat16 [512, 64, 256], P(('req', 'head', 'exp'))
The draws below stay inside these ranges and needn't reach their ends.
Inputs may be any that keep to these rules, and one draw needn't show every extreme that they name: `route_ids`: the 3 ids of a row differ. In each aligned block of 12 rows (the rows of one device) no expert is named by more than 2 rows, a bound that some block reaches.
All inputs are finite; a program needn't handle non-finite values.
Results may differ from the reference program's by a relative error of at most 0.0047.
Values may be sent and summed in bfloat16 or wider, within the bound.
A program may use at most 64 MiB of HBM per device.

```python
import math
import jax
import jax.numpy as jnp
import numpy as np
from jax import lax

D = 7168
FFH = 2560
HEADS = 64
HD = 256
TOPK = 3
TOK_SRC = 12
LEN = 1024
EXPERTS = 24
CAP = 2
TOKENS = 768
REQS = 512


def draw_keys(key, part):
    key = jax.random.fold_in(key, 1)
    samples = jnp.clip(jax.random.normal(key, (REQS, LEN, HD), jnp.float32), -6.0, 6.0)
    return samples.astype(jnp.bfloat16)


def draw_queries(key, part):
    key = jax.random.fold_in(key, 2)
    samples = jnp.clip(jax.random.normal(key, (REQS, HEADS, HD), jnp.float32), -6.0, 6.0)
    return samples.astype(jnp.bfloat16)


def block_levels(own_key, shape, split, smallest, largest):
    loudness = 1.0
    for axis_at, blocks in split:
        steps = jax.random.uniform(jax.random.fold_in(jax.random.fold_in(own_key, 6), axis_at), (blocks,), jnp.float32, smallest / len(split), largest / len(split))
        loudness = loudness * jnp.repeat(jnp.exp(steps), shape[axis_at] // blocks).reshape((-1,) + (1,) * (len(shape) - 1 - axis_at))
    return loudness


def deal_out(rng, own, number, rows, number_of, top, limit, lean):
    sequence = jax.random.permutation(rng, number_of)
    packed, usual = shares(number_of, rows * top, limit, lean, True), shares(number_of, rows * top, limit, lean, False)
    places = jnp.arange(number_of)

    def named(lengths, offset_by):
        used = int((lengths > 0).sum())
        fixed = max(1, used // 4)
        passed = fixed + (places - fixed + offset_by * (used - fixed)) % max(1, number_of - fixed)
        return jnp.zeros((number_of,), jnp.int32).at[sequence[jnp.where(places < fixed, places, passed)]].set(jnp.asarray(lengths, jnp.int32))

    lengths = jnp.where(number % 4 == 0, named(packed, number // 4), named(usual, number - number // 4 - 1))
    mixed = jax.random.permutation(jax.random.fold_in(own, 3), number_of)
    source_of, receiver = mixed[0:number_of // 2 * 2:2], mixed[1:number_of // 2 * 2:2]
    margin = jnp.minimum(lengths[source_of] - 1, limit - lengths[receiver]) // 2
    margin = jnp.where((source_of == sequence[0]) | (receiver == sequence[0]) | (lengths[receiver] == 0), 0, jnp.maximum(margin, 0))
    passed = jax.random.randint(jax.random.fold_in(own, 4), (number_of // 2,), 0, 1 << 20) % (margin + 1)
    lengths = lengths.at[source_of].add(-passed).at[receiver].add(passed)
    members = jnp.searchsorted(jnp.cumsum(lengths), jnp.arange(rows * top), side="right").astype(jnp.int32)
    table = members.reshape(top, rows).T
    table = table[jax.random.permutation(jax.random.fold_in(own, 1), rows)]
    offset_by = jax.random.randint(jax.random.fold_in(own, 2), (rows, 1), 0, top)
    return jnp.take_along_axis(table, (jnp.arange(top)[None, :] + offset_by) % top, axis=1)


def shares(number_of, total, bound, lean, full):
    weights = [(1 << 20) // math.isqrt(grade ** lean) + 1 for grade in range(1, number_of + 1)]
    largest = bound if full else min(bound, max(-(-total // number_of), total * weights[0] // sum(weights)))
    least = 1 if total - largest >= number_of - 1 else 0
    counts, surplus = [largest] + [least] * (number_of - 1), total - largest - least * (number_of - 1)
    while surplus > 0:
        candidates = [i for i in range(1, number_of) if counts[i] < largest] or [i for i in range(1, number_of) if counts[i] < bound]
        mass, budget = sum([weights[i] for i in candidates]), surplus
        for i in candidates:
            extra = min(bound - counts[i], max(1, budget * weights[i] // mass), surplus)
            counts[i] = counts[i] + extra
            surplus = surplus - extra
    return np.array(counts)


def scatter_about(key, shape, scale, reach, cuts=(), kind=jnp.bfloat16):
    values = scale * jax.random.normal(key, shape, jnp.float32)
    if cuts:
        values = values * block_levels(key, shape, cuts, -0.22, 0.18)
    return jnp.clip(values, -reach, reach).astype(kind)


def setup_inputs(seed: int = 0) -> dict:
    streams_of = jax.random.split(jax.random.key(seed), 9)
    moe_input = scatter_about(streams_of[0], (TOKENS, D), 1.0, 6.0, ((0, 64), (1, 8)))
    route_ids_keys = jax.random.split(jax.random.fold_in(streams_of[1], 1), TOKENS // TOK_SRC)
    route_ids_turns = jax.random.permutation(jax.random.fold_in(streams_of[1], 3), TOKENS // TOK_SRC)
    route_ids = jax.vmap(lambda own, number: deal_out(jax.random.fold_in(streams_of[1], 2), own, number, TOK_SRC, EXPERTS, TOPK, CAP, 2))(route_ids_keys, route_ids_turns).reshape((TOKENS, TOPK))
    route_weight = jnp.clip(0.1 + 0.9 * jax.random.uniform(streams_of[2], (TOKENS, TOPK), jnp.float32) ** block_levels(streams_of[2], (TOKENS, TOPK), ((0, 64),), -0.2, 0.2), 0.1, 1.0)
    w_up = scatter_about(streams_of[3], (EXPERTS, FFH, D), D ** -0.5, 0.0625, ((0, 8), (1, 64)))
    w_down = scatter_about(streams_of[4], (EXPERTS, FFH, D), FFH ** -0.5, 0.125, ((0, 8), (2, 64)))
    queries = draw_queries(jax.random.fold_in(streams_of[8], 71), 0)
    keys = draw_keys(jax.random.fold_in(streams_of[8], 71), 0)
    values = scatter_about(streams_of[7], (REQS, LEN, HD), 1.0, 6.0, ((0, 512),))
    return {"moe_input": moe_input, "route_ids": route_ids, "route_weight": route_weight, "w_up": w_up, "w_down": w_down, "queries": queries, "keys": keys, "values": values}


def reference(moe_input, route_ids, route_weight, w_up, w_down, queries, keys, values):
    onehot = (route_ids[:, :, None] == jnp.arange(EXPERTS, dtype=jnp.int32)[None, None, :]).astype(jnp.int32)
    per_row = onehot.sum(axis=1)
    blocks = per_row.reshape(TOKENS // TOK_SRC, TOK_SRC, EXPERTS)
    before = (jnp.cumsum(blocks, axis=1) - blocks).reshape(TOKENS, EXPERTS)
    slot_rank = lax.optimization_barrier(jnp.sum(onehot * before[:, None, :], axis=2)).astype(jnp.int32)
    block_id = (jnp.arange(TOKENS, dtype=jnp.int32) // TOK_SRC).astype(jnp.int32)
    slot = (block_id[:, None] * CAP + slot_rank).astype(jnp.int32)
    slot_count = TOKENS // TOK_SRC * CAP
    spread = jnp.broadcast_to(moe_input[:, None, :], (TOKENS, TOPK, D))
    dispatched = jnp.zeros((EXPERTS, slot_count, D), jnp.bfloat16).at[route_ids, slot].set(spread)

    def one_expert(operands):
        slots_in, up_rows, down_rows = operands
        raised = jnp.dot(slots_in, up_rows.T, preferred_element_type=jnp.float32)
        activated = jax.nn.silu(raised).astype(jnp.bfloat16)
        return jnp.dot(activated, down_rows, preferred_element_type=jnp.float32).astype(jnp.bfloat16)
    expert_out = lax.map(one_expert, (dispatched, w_up, w_down))
    picked = expert_out[route_ids, slot].astype(jnp.float32)
    expert_sum = lax.optimization_barrier(jnp.sum(route_weight[:, :, None].astype(jnp.float32) * picked, axis=1))
    moe_output = (moe_input.astype(jnp.float32) + expert_sum).astype(jnp.bfloat16)
    scores = jnp.einsum('rhd,rld->rhl', queries.astype(jnp.float32), keys.astype(jnp.float32)) / math.sqrt(HD)
    row_max = lax.optimization_barrier(jnp.max(scores, axis=2, keepdims=True))
    weights = jnp.exp(scores - row_max)
    row_total = lax.optimization_barrier(jnp.sum(weights, axis=2))
    rounded = weights.astype(jnp.bfloat16)
    weighted = jnp.einsum('rhl,rld->rhd', rounded.astype(jnp.float32), values.astype(jnp.float32))
    context = (weighted / row_total[:, :, None]).astype(jnp.bfloat16)
    return (moe_output, context)
```

```python
import functools
import math

import jax
import jax.numpy as jnp
from jax import lax
from jax.experimental import pallas as pl
from jax.experimental.pallas import tpu as pltpu
from jax.sharding import PartitionSpec as P

BF = jnp.bfloat16
F32 = jnp.float32
I32 = jnp.int32
NT = (((1,), (1,)), ((), ()))


def iota(shape, dim):
    return lax.broadcasted_iota(I32, shape, dim)


def onehot(match):
    return jnp.where(match, 1.0, 0.0).astype(BF)


def dot(a, b):
    return jnp.dot(a, b, preferred_element_type=F32)


def attend(q, k, v):
    scores = lax.dot_general(q, k, NT, preferred_element_type=F32) * (1.0 / math.sqrt(q.shape[1]))
    weights = jnp.exp(scores - jnp.max(scores, axis=1, keepdims=True))
    total = jnp.sum(weights, axis=1, keepdims=True)
    return (dot(weights.astype(BF), v) / total).astype(BF)


def kernel(
    n,
    ids_ref, wt_ref, x_ref, q_ref, k_hbm, v_hbm, up_hbm, down_hbm,
    out_ref, ctx_ref,
    k_ref, v_ref, down_ref, up_ref, upcat_ref, wd_ref,
    tok_ref, named_ref, send1_ref, recv1_ref, xg_ref, part_ref, partin_ref,
    hg_ref, acc_ref, r1s_ref, r1r_ref, r2s_ref, r2r_ref,
    loc_sem, up_s, up_r, s1_s, s1_r, s2_s, s2_r, s3_s, s3_r, pt_s, pt_r,
    hz_s, hz_r, hg_s, hg_r, ho_s, ho_r, r1_s, r1_r, r2_s, r2_r,
):
    toks, width = x_ref.shape
    dq = 2 * width
    half = send1_ref.shape[1]
    fs = up_ref.shape[2]
    dn = down_ref.shape[2]
    g2 = 2 * n
    unit = 12 * n
    rows = 2 * n * n * n
    plane = n * n
    column = 2 * plane

    req, zl, ex = lax.axis_index("req"), lax.axis_index("head"), lax.axis_index("exp")
    y, x = req // n, req % n
    zh, c = ex // 2, ex % 2
    g = x * (1 - c) + y * c
    o = y * (1 - c) + x * c

    def rid(g_, o_, c_):
        return (o_ * (1 - c_) + g_ * c_) * n + g_ * (1 - c_) + o_ * c_

    def dev(r_, zl_, ex_):
        return {"req": r_, "head": zl_, "exp": ex_}

    def remote(src, dst, ss, rs, where):
        return pltpu.make_async_remote_copy(
            src_ref=src, dst_ref=dst, send_sem=ss, recv_sem=rs,
            device_id=where, device_id_type=pl.DeviceIdType.MESH,
        )

    def add(v, d, m=n):
        return (v + d) % m

    sends = []

    load_down = pltpu.make_async_copy(down_hbm, down_ref, loc_sem.at[0])
    load_k = pltpu.make_async_copy(k_hbm, k_ref, loc_sem.at[1])
    load_v = pltpu.make_async_copy(v_hbm, v_ref, loc_sem.at[2])
    load_up = pltpu.make_async_copy(up_hbm.at[:, :, pl.ds(g * dq, dq)], up_ref.at[g], loc_sem.at[3])
    load_up.start()
    load_k.start()
    load_v.start()
    load_down.start()

    barrier = pltpu.get_barrier_semaphore()

    def greet(where):
        pl.semaphore_signal(barrier, inc=1, device_id=where, device_id_type=pl.DeviceIdType.MESH)

    def greet_plane(d, carry):
        greet(dev(add(req, d, plane), zl, ex))
        return carry

    def greet_column(d, carry):
        m = add(zl * g2 + ex, d, column)
        greet(dev(req, m // g2, m % g2))
        return carry

    lax.fori_loop(1, plane, greet_plane, 0)
    lax.fori_loop(1, column, greet_column, 0)

    targets = []
    for dt in range(2):
        t = (c + dt) % 2
        g_t = x * (1 - t) + y * t
        o_t = y * (1 - t) + x * t
        for dz in range(n):
            zt = add(zh, dz)
            targets.append((t, g_t, zt, dev(rid(zh, o_t, t), zl, zt * 2 + t), dt == 0 and dz == 0))
    home = g == zh
    for t, g_t, zt, where, own in targets:
        if own:
            @pl.when(jnp.logical_not(home))
            def _():
                greet(where)
        else:
            greet(where)
    for dt in range(2):
        cs = (c + dt) % 2
        for dg in range(n):
            gs = add(g, dg)
            where = dev(rid(gs, o, c), zl, g * 2 + cs)
            if dt == 0 and dg == 0:
                @pl.when(jnp.logical_not(home))
                def _():
                    greet(where)
            else:
                greet(where)

    lanes = g2 * 16
    lane = iota((1, lanes), 1)
    low = lane % 8
    lane_expert = jnp.where(low < 6, (lane // 16) * 3 + low // 2, -1)
    ids = ids_ref[...]
    wts = wt_ref[...]
    named = jnp.zeros((toks, lanes), F32)
    weight = jnp.zeros((toks, lanes), F32)
    for kk in range(3):
        hit = ids[:, kk:kk + 1] == lane_expert
        named = named + jnp.where(hit, 1.0, 0.0)
        weight = weight + jnp.where(hit, wts[:, kk:kk + 1], 0.0)
    named_ref[...] = jnp.zeros_like(named_ref)
    named_ref[0, 0:toks, :] = named
    named_ref[1, 0:toks, :] = weight
    tok_ref[...] = jnp.zeros_like(tok_ref)
    tok_ref[0:toks, 0:width] = x_ref[...]
    named = named_ref[0]
    tri = onehot(iota((16, 16), 0) > iota((16, 16), 1))
    before = dot(tri, named.astype(BF))
    pick = jnp.where(before == (lane % 2).astype(F32), named, 0.0)
    comb = pick * named_ref[1]
    spread = dot(pick.T.astype(BF), tok_ref[...])
    upper = (iota((lanes, 1), 0) % 16) >= 8
    send1_ref[...] = jnp.where(upper, spread[:, half:], spread[:, :half]).astype(BF)

    @pl.when(home)
    def _():
        pl.semaphore_wait(barrier, plane - 1 + column - 1 + 2 * (2 * n - 1))

    @pl.when(jnp.logical_not(home))
    def _():
        pl.semaphore_wait(barrier, plane - 1 + column - 1 + 2 * (2 * n))

    firsts = []
    for at, (t, g_t, zt, where, own) in enumerate(targets):
        src = send1_ref.at[pl.ds((zt * 2 + t) * 16, 16), :]
        place = c * n + g_t
        dst = recv1_ref.at[pl.ds(place * 16, 16), :]
        cp = remote(src, dst, s1_s.at[at], s1_r.at[place], where)
        firsts.append(cp)
        if own:
            @pl.when(home)
            def _():
                pltpu.make_async_copy(src, dst, s1_r.at[place]).start()

            @pl.when(jnp.logical_not(home))
            def _():
                cp.start()
        else:
            cp.start()
            sends.append(cp)

    ups = []
    for d in range(1, n):
        p = add(g, d)
        cp = remote(
            up_hbm.at[:, :, pl.ds(p * dq, dq)], up_ref.at[g], up_s.at[d], up_r.at[d],
            dev(rid(p, o, c), zl, ex),
        )
        cp.start()
        ups.append(cp)
        sends.append(cp)

    load_k.wait()
    load_v.wait()
    ctx_ref[...] = attend(q_ref[...], k_ref[...], v_ref[...])

    for i in range(2 * n):
        ref = recv1_ref.at[pl.ds(i * 16, 16), :]
        pltpu.make_async_copy(ref, ref, s1_r.at[i]).wait()

    ru = iota((unit, 2 * n * 16), 0)
    second = jnp.where(ru >= 6 * n, 1, 0)
    rest = ru - 6 * n * second
    origin = (second * n + (rest % g2) // 2) * 16 + (rest // g2) * 2 + rest % 2
    col = iota((unit, 2 * n * 16), 1)
    got = recv1_ref[...]
    left = dot(onehot(col == origin), got).astype(BF)
    right = dot(onehot(col == origin + 8), got).astype(BF)
    xg_ref[o, zl, :, 0:half] = left
    xg_ref[o, zl, :, half:width] = right[:, 0:width - half]

    def around(piece, ss, rs):
        for d in range(1, n):
            cp = remote(piece, piece, ss.at[d], rs.at[d], dev(rid(g, add(o, d), c), zl, ex))
            cp.start()
            sends.append(cp)

    for d in (list(range(1, n))):
        own = xg_ref.at[o, zl]
        cp = remote(own, own, s2_s.at[d], s2_r.at[d], dev(req, add(zl, d), ex))
        cp.start()
        sends.append(cp)
    around(xg_ref.at[o, zl], s3_s.at[0], s3_r.at[0])

    load_down.wait()
    wd_ref[...] = jnp.zeros_like(wd_ref)

    def spread_down(i, carry):
        for k in range(3):
            both = down_ref[k, pl.ds(pl.multiple_of(i * 2 * fs, 16), 2 * fs), :].astype(F32)
            for side in range(2):
                piece = both[side * fs:(side + 1) * fs]
                parts = [piece]
                if k:
                    parts = [jnp.zeros((k * fs, dn), F32)] + parts
                parts.append(jnp.zeros((128 - (k + 1) * fs, dn), F32))
                wd_ref[i, side * 128:(side + 1) * 128, k * 128:k * 128 + dn] = jnp.concatenate(
                    parts, axis=0).astype(BF)
        return carry

    lax.fori_loop(0, n * n * n // 2, spread_down, 0)

    for dz in range(1, n):
        piece = xg_ref.at[o, add(zl, n - dz)]
        pltpu.make_async_copy(piece, piece, s2_r.at[dz]).wait()
        around(piece, s3_s.at[dz], s3_r.at[dz])

    def fix_up(p):
        for h in range(2):
            parts = [up_ref[p, k, :, h * width:(h + 1) * width].astype(F32) for k in range(3)]
            parts.append(jnp.zeros((128 - 3 * fs, width), F32))
            upcat_ref[p, h * 128:(h + 1) * 128, :] = jnp.concatenate(parts, axis=0).astype(BF)

    load_up.wait()
    fix_up(g)
    for d in range(1, n):
        p = add(g, n - d)
        pltpu.make_async_copy(up_ref.at[p], up_ref.at[p], up_r.at[d]).wait()
        fix_up(p)

    band = iota((1, 1, 128), 2)
    for d in range(n):
        os = add(o, n - d)
        if d:
            for dz in range(n):
                piece = xg_ref.at[os, add(zl, n - dz)]
                pltpu.make_async_copy(piece, piece, s3_r.at[dz, d]).wait()

        def products(p, carry):
            a = xg_ref[os].reshape(n * unit, width)
            r = lax.dot_general(a, upcat_ref[p], NT, preferred_element_type=F32)
            r = r.reshape(n, unit, 256)
            total = jnp.zeros((n, g2, 128), F32)
            for h in range(2):
                rk = [
                    r[:, (3 * h + k) * g2:(3 * h + k + 1) * g2, h * 128:(h + 1) * 128]
                    for k in range(3)
                ]
                total = total + jnp.where(
                    band < fs, rk[0], jnp.where(band < 2 * fs, rk[1], rk[2]))
            part_ref[p, os] = total.reshape(n * g2, 128)
            return carry

        lax.fori_loop(0, n, products, 0)

    for d in range(1, n):
        p = add(g, d)
        cp = remote(part_ref.at[p], partin_ref.at[d - 1], pt_s.at[d], pt_r.at[d], dev(rid(p, o, c), zl, ex))
        cp.start()
        sends.append(cp)
    raised = part_ref[g]
    for d in range(1, n):
        ref = partin_ref.at[d - 1]
        pltpu.make_async_copy(ref, ref, pt_r.at[d]).wait()
        raised = raised + partin_ref[d - 1]
    raised = raised.reshape(rows, 128)
    hidden = (raised / (1.0 + jnp.exp(-raised))).astype(BF)
    rn = iota((rows, rows), 0)
    src = ((rn // (g2 * n)) * n + (rn % g2) // 2) * g2 + ((rn // g2) % n) * 2 + rn % 2
    hidden = dot(onehot(iota((rows, rows), 1) == src), hidden).astype(BF)

    def hpiece(g_, o_, z_):
        return hg_ref.at[g_, o_, :, pl.ds(z_ * 128, 128)]

    hg_ref[g, o, :, pl.ds(pl.multiple_of(zl * 128, 128), 128)] = hidden

    def hgroup(dz):
        piece = hpiece(g, o, add(zl, n - dz))
        for d in range(1, n):
            cp = remote(piece, piece, hg_s.at[dz, d], hg_r.at[dz, d], dev(rid(add(g, d), o, c), zl, ex))
            cp.start()
            sends.append(cp)

    def hother(dg):
        piece = hg_ref.at[add(g, n - dg), o]
        for d in range(1, n):
            cp = remote(piece, piece, ho_s.at[dg, d], ho_r.at[dg, d], dev(rid(g, add(o, d), c), zl, ex))
            cp.start()
            sends.append(cp)

    own = hpiece(g, o, zl)
    for d in range(1, n):
        cp = remote(own, own, hz_s.at[d], hz_r.at[d], dev(req, add(zl, d), ex))
        cp.start()
        sends.append(cp)
    hgroup(0)
    for dz in range(1, n):
        piece = hpiece(g, o, add(zl, n - dz))
        pltpu.make_async_copy(piece, piece, hz_r.at[dz]).wait()
        hgroup(dz)
    hother(0)

    def lower(g_, o_):
        r_ = rid(g_, o_, c)
        w = wd_ref[pl.ds(r_ * (n // 2), n // 2)].reshape(n * 128, 384)
        acc_ref[...] += dot(hg_ref[g_, o_], w)

    acc_ref[...] = jnp.zeros_like(acc_ref)
    lower(g, o)
    for dg in range(1, n):
        gs = add(g, n - dg)
        for dz in range(n):
            piece = hpiece(gs, o, add(zl, n - dz))
            pltpu.make_async_copy(piece, piece, hg_r.at[dz, dg]).wait()
        hother(dg)
        lower(gs, o)
    for dg in range(n):
        gs = add(g, n - dg)
        for d in range(1, n):
            os = add(o, n - d)
            piece = hg_ref.at[gs, os]
            pltpu.make_async_copy(piece, piece, ho_r.at[dg, d]).wait()
            lower(gs, os)

    acc = acc_ref[...].reshape(plane, g2, 384)
    if g2 < 8:
        acc = jnp.concatenate([acc, jnp.zeros((plane, 8 - g2, 384), F32)], axis=1)
    lower_rows = jnp.concatenate([acc[:, :, 256:384], jnp.zeros((plane, 8, 128), F32)], axis=2)
    r1s_ref[...] = jnp.concatenate([acc[:, :, 0:256], lower_rows], axis=1).astype(BF)
    spot = o * n + g

    def r1_send(d, carry):
        i = add(spot, d, plane)
        remote(
            r1s_ref.at[i], r1r_ref.at[req], r1_s.at[0], r1_r.at[0],
            dev(rid(i % n, i // n, c), zl, ex),
        ).start()
        return carry

    lax.fori_loop(1, plane, r1_send, 0)
    r1r_ref[req] = r1s_ref[spot]

    hn = n // 2
    mr = hn * 8
    rr = iota((column * mr, plane * 16), 0)
    m = rr // mr
    xi = (rr % mr) // 8
    k2 = (rr % 8) // 2
    e2 = m % g2
    srcx = (e2 // 2) * n + (e2 % 2) * hn + xi
    origin = srcx * 16 + (k2 // 2) * 8 + (m // g2) * 2 + rr % 2
    same = iota((column * mr, plane * 16), 1) == origin
    take_a = onehot(jnp.logical_and(same, jnp.logical_or(k2 == 0, k2 == 2)))
    take_b = onehot(jnp.logical_and(same, k2 == 1))

    others = r1r_ref.at[pl.ds(0, plane - 1)]
    pltpu.make_async_copy(others, others, r1_r.at[0]).wait()
    got = r1r_ref[...].reshape(plane * 16, 256)
    r2s_ref[...] = (dot(take_a, got[:, 0:128]) + dot(take_b, got[:, 128:256])).astype(BF).reshape(
        column, mr, 128)
    spot2 = zl * g2 + ex

    def r2_dst():
        return r2r_ref.at[pl.ds(ex * mr, mr), pl.ds(zl * 128, 128)]

    def r2_send(d, carry):
        i = add(spot2, d, column)
        remote(r2s_ref.at[i], r2_dst(), r2_s.at[0], r2_r.at[0], dev(req, i // g2, i % g2)).start()
        return carry

    lax.fori_loop(1, column, r2_send, 0)
    keep = pltpu.make_async_copy(r2s_ref.at[spot2], r2_dst(), loc_sem.at[4])
    keep.start()
    keep.wait()
    others = r2s_ref.at[pl.ds(0, column - 1)]
    pltpu.make_async_copy(others, others, r2_r.at[0]).wait()

    cut = lane % 16
    both = []
    for xi_at in range(hn):
        both.append(jnp.where(cut // 8 == xi_at, comb, 0.0))
    both = jnp.concatenate(both, axis=0)
    if mr < 16:
        both = both.reshape(16 * hn, g2, 16)[:, :, 0:mr].reshape(16 * hn, g2 * mr)
    p0 = both.astype(BF)
    left_over = both - p0.astype(F32)
    p1 = left_over.astype(BF)
    p2 = (left_over - p1.astype(F32)).astype(BF)
    got = r2r_ref[...]
    sums = dot(p0, got) + (dot(p1, got) + dot(p2, got))
    pieces = []
    for xi_at in range(hn):
        for z in range(n):
            pieces.append(sums[xi_at * 16:xi_at * 16 + toks, z * 128:z * 128 + dn])
    total = jnp.concatenate(pieces, axis=1)
    out_ref[...] = (x_ref[...].astype(F32) + total).astype(BF)

    for cp in sends:
        cp.wait_send()

    @pl.when(jnp.logical_not(home))
    def _():
        firsts[0].wait_send()
    others = r1s_ref.at[pl.ds(0, plane - 1)]
    pltpu.make_async_copy(others, others, r1_s.at[0]).wait()
    others = r2s_ref.at[pl.ds(0, column - 1)]
    pltpu.make_async_copy(others, others, r2_s.at[0]).wait()


def shards(moe_input, route_ids, route_weight, w_up, w_down, queries, keys, values):
    n = lax.axis_size("head")
    toks, width = moe_input.shape
    fs = w_up.shape[1]
    dn = w_down.shape[2]
    ffh = w_down.shape[1]
    heads, hd = queries.shape[1:]
    length = keys.shape[1]
    dq = 2 * width
    half = -(-width // 256) * 128
    rows = 2 * n * n * n
    plane, column = n * n, 2 * n * n
    mr = (n // 2) * 8
    vm = pl.BlockSpec(memory_space=pltpu.VMEM)
    hbm = pl.BlockSpec(memory_space=pl.ANY)
    dma = pltpu.SemaphoreType.DMA
    moe, ctx = pl.pallas_call(
        functools.partial(kernel, n),
        out_shape=(
            jax.ShapeDtypeStruct((toks, width), BF),
            jax.ShapeDtypeStruct((heads, hd), BF),
        ),
        in_specs=[vm, vm, vm, vm, hbm, hbm, hbm, hbm],
        out_specs=(vm, vm),
        scratch_shapes=[
            pltpu.VMEM((length, hd), BF),
            pltpu.VMEM((length, hd), BF),
            pltpu.VMEM((3, ffh, dn), BF),
            pltpu.VMEM((n, 3, fs, dq), BF),
            pltpu.VMEM((n, 256, width), BF),
            pltpu.VMEM((n * n * n // 2, 256, 384), BF),
            pltpu.VMEM((16, 2 * half), BF),
            pltpu.VMEM((2, 16, 32 * n), F32),
            pltpu.VMEM((32 * n, half), BF),
            pltpu.VMEM((32 * n, half), BF),
            pltpu.VMEM((n, n, 12 * n, width), BF),
            pltpu.VMEM((n, n, 2 * n * n, 128), F32),
            pltpu.VMEM((n - 1, n, 2 * n * n, 128), F32),
            pltpu.VMEM((n, n, rows, n * 128), BF),
            pltpu.VMEM((rows, 384), F32),
            pltpu.VMEM((plane, 16, 256), BF),
            pltpu.VMEM((plane, 16, 256), BF),
            pltpu.VMEM((column, mr, 128), BF),
            pltpu.VMEM((2 * n * mr, n * 128), BF),
            dma((5,)),
            dma((n,)), dma((n,)),
            dma((2 * n,)), dma((2 * n,)),
            dma((n,)), dma((n,)),
            dma((n, n)), dma((n, n)),
            dma((n,)), dma((n,)),
            dma((n,)), dma((n,)),
            dma((n, n)), dma((n, n)),
            dma((n, n)), dma((n, n)),
            dma((1,)), dma((1,)),
            dma((1,)), dma((1,)),
        ],
        compiler_params=pltpu.CompilerParams(
            collective_id=0, has_side_effects=True, vmem_limit_bytes=48 * 1024 * 1024
        ),
        cost_estimate=pl.CostEstimate(flops=10**9, bytes_accessed=10**7, transcendentals=10**5),
        name="decode",
    )(route_ids, route_weight, moe_input, queries[0], keys[0], values[0], w_up, w_down)
    return (moe, ctx[None])


def solution(mesh):
    placed = (
        P(("req", "head"), "exp"),
        P(("req", "head"), None),
        P(("req", "head"), None),
        P("exp", ("req", "head"), None),
        P("exp", None, ("req", "head")),
        P(("req", "head", "exp"), None, None),
        P(("req", "head", "exp"), None, None),
        P(("req", "head", "exp"), None, None),
    )
    return jax.shard_map(
        shards,
        mesh=mesh,
        in_specs=placed,
        out_specs=(P(("req", "head"), "exp"), P(("req", "head", "exp"), None, None)),
        check_vma=False,
    )
```

```python
import functools
import math

import jax
import jax.numpy as jnp
from jax import lax
from jax.experimental import pallas as pl
from jax.experimental.pallas import tpu as pltpu
from jax.sharding import PartitionSpec as P

BF = jnp.bfloat16
F32 = jnp.float32
I32 = jnp.int32
NT = (((1,), (1,)), ((), ()))


def iota(shape, dim):
    return lax.broadcasted_iota(I32, shape, dim)


def onehot(match):
    return jnp.where(match, 1.0, 0.0).astype(BF)


def dot(a, b):
    return jnp.dot(a, b, preferred_element_type=F32)


def attend(q, k, v):
    scores = lax.dot_general(q, k, NT, preferred_element_type=F32) * (1.0 / math.sqrt(q.shape[1]))
    weights = jnp.exp(scores - jnp.max(scores, axis=1, keepdims=True))
    total = jnp.sum(weights, axis=1, keepdims=True)
    return (dot(weights.astype(BF), v) / total).astype(BF)


def kernel(
    n, nz,
    ids_ref, wt_ref, x_hbm, q_hbm, k_hbm, v_hbm, up_hbm, down_hbm,
    out_ref, ctx_ref,
    x_ref, q_ref, k_ref, v_ref, down_ref, up_ref, upcat_ref, wd_ref,
    tok_ref, ids_pad, send1_ref, recv1_ref, xg_ref, part_ref, partin_ref,
    hg_ref, acc_ref, r1s_ref, r1r_ref, r2r_ref,
    loc_sem, up_s, up_r, s1_s, s1_r, s2_s, s2_r, s3_s, s3_r,
    pt_s, pt_r, hz_s, hz_r, hg_s, hg_r, ho_s, ho_r,
    r1_s, r1_r, r2_s, r2_r,
):
    toks, width = x_ref.shape
    dq = 2 * width
    chunks = width // 128
    fs = up_ref.shape[2]
    dn = down_ref.shape[1]
    g2 = 2 * n
    unit = 12 * n
    rows = 2 * n * n * nz
    plane = n * n
    column = g2 * nz
    srcs = plane * nz
    hops = (2, 1, 3) if n == 4 else (1,)

    req, zl, ex = lax.axis_index("req"), lax.axis_index("head"), lax.axis_index("exp")
    y, x = req // n, req % n
    zh, c = ex // 2, ex % 2
    g = x * (1 - c) + y * c
    o = y * (1 - c) + x * c

    def rid(g_, o_, c_):
        return (o_ * (1 - c_) + g_ * c_) * n + g_ * (1 - c_) + o_ * c_

    def dev(r_, zl_, ex_):
        return {"req": r_, "head": zl_, "exp": ex_}

    def remote(src, dst, ss, rs, where):
        return pltpu.make_async_remote_copy(
            src_ref=src, dst_ref=dst, send_sem=ss, recv_sem=rs,
            device_id=where, device_id_type=pl.DeviceIdType.MESH,
        )

    def arrived(ref, sem):
        pltpu.make_async_copy(ref, ref, sem).wait()

    def add(v, d, m=n):
        return (v + d) % m

    sends = []

    def send(src, dst, ss, rs, where):
        cp = remote(src, dst, ss, rs, where)
        cp.start()
        sends.append(cp)

    def at_group(d):
        return dev(rid(add(g, d), o, c), zl, ex)

    def at_other(d):
        return dev(rid(g, add(o, d), c), zl, ex)

    def spread(block, where, ss, rs):
        for d in hops:
            send(block, block, ss.at[d], rs.at[d], where(d))

    loads = [
        (x_hbm, x_ref), (q_hbm, q_ref), (k_hbm, k_ref), (v_hbm, v_ref),
        (up_hbm.at[:, :, pl.ds(g * dq, dq)], up_ref.at[g]), (down_hbm, down_ref),
    ]
    loads = [pltpu.make_async_copy(a, b, loc_sem.at[i]) for i, (a, b) in enumerate(loads)]
    for cp in loads:
        cp.start()
    load_x, load_q, load_k, load_v, load_up, load_down = loads

    barrier = pltpu.get_barrier_semaphore()

    def greet(where):
        pl.semaphore_signal(barrier, inc=1, device_id=where, device_id_type=pl.DeviceIdType.MESH)

    def greet_plane(d, carry):
        greet(dev(add(req, d, plane), zl, ex))
        return carry

    def greet_column(d, carry):
        m = add(zl * g2 + ex, d, column)
        greet(dev(req, m // g2, m % g2))
        return carry

    lax.fori_loop(1, column, greet_column, 0)
    lax.fori_loop(1, plane, greet_plane, 0)

    targets = []
    for dz in hops + (0,):
        for dt in range(2):
            t = (c + dt) % 2
            g_t = x * (1 - t) + y * t
            o_t = y * (1 - t) + x * t
            zt = add(zh, dz)
            targets.append((t, g_t, zt, dev(rid(zh, o_t, t), zl, zt * 2 + t), dt == 0 and dz == 0))
    home = g == zh
    for t, g_t, zt, where, own in targets:
        if own:
            @pl.when(jnp.logical_not(home))
            def _():
                greet(where)
        else:
            greet(where)
    for dt in range(2):
        cs = (c + dt) % 2
        for dg in range(n):
            gs = add(g, dg)
            where = dev(rid(gs, o, c), zl, g * 2 + cs)
            if dt == 0 and dg == 0:
                @pl.when(jnp.logical_not(home))
                def _():
                    greet(where)
            else:
                greet(where)

    ids_pad[...] = jnp.zeros_like(ids_pad)
    ids_pad[0:3, 0:toks] = (ids_ref[...] + 1).astype(F32)
    hn = n // 2
    mr = hn * 8
    r128, c128 = iota((128, 128), 0), iota((128, 128), 1)
    tile = onehot(jnp.logical_and(c128 % 16 == r128, r128 < 16))
    tiled = dot(ids_pad[...].astype(BF), tile).astype(I32)
    tri = onehot(jnp.logical_and(r128 // 16 == c128 // 16, r128 % 16 < c128 % 16))
    grp = lax.broadcasted_iota(I32, (g2, 48, 128), 0)
    sub = lax.broadcasted_iota(I32, (g2, 48, 128), 1)
    lane = lax.broadcasted_iota(I32, (g2, 48, 128), 2)
    here = (lane // 16 == sub % 8).reshape(g2 * 48, 128)
    expert = (grp * 3 + sub // 16 + 1).reshape(g2 * 48, 128)
    slot = ((sub // 8) % 2).astype(F32).reshape(g2 * 48, 128)
    named = jnp.zeros((g2 * 48, 128), F32)
    for kk in range(3):
        hit = jnp.logical_and(here, tiled[kk:kk + 1, :] == expert)
        named = named + jnp.where(hit, 1.0, 0.0)
    before = dot(named.astype(BF), tri)
    pick = jnp.where(before == slot, named, 0.0).astype(BF)
    tok_ref[...] = jnp.zeros_like(tok_ref)
    load_x.wait()
    for ch in range(chunks):
        tok_ref[ch * 16:ch * 16 + toks, :] = x_ref[:, ch * 128:(ch + 1) * 128]
    send1_ref[...] = dot(pick, tok_ref[...]).astype(BF)

    @pl.when(home)
    def _():
        pl.semaphore_wait(barrier, plane - 1 + column - 1 + 2 * (2 * n - 1))

    @pl.when(jnp.logical_not(home))
    def _():
        pl.semaphore_wait(barrier, plane - 1 + column - 1 + 2 * (2 * n))

    first = None
    for at, (t, g_t, zt, where, own) in enumerate(targets):
        src = send1_ref.at[pl.ds((zt * 2 + t) * 48, 48), :]
        place = c * n + g_t
        dst = recv1_ref.at[pl.ds(place * 48, 48), :]
        cp = remote(src, dst, s1_s.at[at], s1_r.at[place], where)
        if own:
            first = cp

            @pl.when(home)
            def _():
                pltpu.make_async_copy(src, dst, s1_r.at[place]).start()

            @pl.when(jnp.logical_not(home))
            def _():
                cp.start()
        else:
            cp.start()
            sends.append(cp)

    for d in hops:
        send(
            up_hbm.at[:, :, pl.ds(add(g, d) * dq, dq)], up_ref.at[g],
            up_s.at[d], up_r.at[d], at_group(d),
        )

    load_q.wait()
    load_k.wait()
    load_v.wait()
    ctx_ref[...] = attend(q_ref[...], k_ref[...], v_ref[...])

    batch = min(16, srcs)

    def spread_down(i):
        for k in range(3):
            t = down_ref[k, :, i * batch * fs:(i + 1) * batch * fs].astype(F32).T
            for s in range(batch):
                parts = [t[s * fs:(s + 1) * fs]]
                if k:
                    parts = [jnp.zeros((k * fs, dn), F32)] + parts
                parts.append(jnp.zeros((128 - (k + 1) * fs, dn), F32))
                at = (i * batch + s) * 128
                wd_ref[at:at + 128, k * 128:k * 128 + dn] = jnp.concatenate(parts, axis=0).astype(BF)

    ru = lax.broadcasted_iota(I32, (chunks, unit, g2 * 48), 1)
    ch = lax.broadcasted_iota(I32, (chunks, unit, g2 * 48), 0)
    col = lax.broadcasted_iota(I32, (chunks, unit, g2 * 48), 2)
    second = jnp.where(ru >= 6 * n, 1, 0)
    rest = ru - 6 * n * second
    origin = (second * n + (rest % g2) // 2) * 48 + (rest // g2) * 16 + (rest % 2) * 8 + ch
    order = onehot(col == origin).reshape(chunks * unit, g2 * 48)
    for i in range(g2):
        arrived(recv1_ref.at[pl.ds(i * 48, 48), :], s1_r.at[i])
    placed = dot(order, recv1_ref[...]).astype(BF)
    for ch in range(chunks):
        xg_ref[o, zl, :, ch * 128:(ch + 1) * 128] = placed[ch * unit:(ch + 1) * unit]

    own = xg_ref.at[o, zl]
    for d in range(1, nz):
        send(own, own, s2_s.at[d], s2_r.at[d], dev(req, add(zl, d, nz), ex))

    def x_from(dz):
        return lambda d: xg_ref.at[add(o, d), add(zl, nz - dz, nz)]

    spread(own, at_other, s3_s.at[0], s3_r.at[0])
    load_down.wait()
    wd_ref[...] = jnp.zeros_like(wd_ref)
    batches = srcs // batch
    for i in range((batches + 1) // 2):
        spread_down(i)
    for dz in range(1, nz):
        block = x_from(dz)(0)
        arrived(block, s2_r.at[dz])
        spread(block, at_other, s3_s.at[dz], s3_r.at[dz])

    def fix_up(p):
        for h in range(2):
            parts = [up_ref[p, k, :, h * width:(h + 1) * width].astype(F32) for k in range(3)]
            parts.append(jnp.zeros((128 - 3 * fs, width), F32))
            upcat_ref[p, h * 128:(h + 1) * 128, :] = jnp.concatenate(parts, axis=0).astype(BF)

    load_up.wait()
    fix_up(g)
    for d in hops:
        p = add(g, n - d)
        arrived(up_ref.at[p], up_r.at[d])
        fix_up(p)

    band = iota((1, 1, 128), 2)

    def products(p, zs):
        a = xg_ref[:, zs].reshape(n * unit, width)
        r = lax.dot_general(a, upcat_ref[p], NT, preferred_element_type=F32)
        r = r.reshape(n, unit, 256)
        total = jnp.zeros((n, g2, 128), F32)
        for h in range(2):
            rk = [
                r[:, (3 * h + k) * g2:(3 * h + k + 1) * g2, h * 128:(h + 1) * 128]
                for k in range(3)
            ]
            total = total + jnp.where(band < fs, rk[0], jnp.where(band < 2 * fs, rk[1], rk[2]))
        part_ref[p, :, zs] = total

    for dz in range(nz):
        for d in hops:
            arrived(x_from(dz)(n - d), s3_r.at[dz, d])
        zs = add(zl, nz - dz, nz)
        for d in hops:
            p = add(g, d)
            products(p, zs)
            send(
                part_ref.at[p, :, zs], partin_ref.at[d - 1, :, zs],
                pt_s.at[dz, d], pt_r.at[dz, d], at_group(d),
            )
        products(g, zs)

    for i in range((batches + 1) // 2, batches):
        spread_down(i)

    raised = part_ref[g]
    for d in hops:
        for dz in range(nz):
            arrived(partin_ref.at[d - 1, :, add(zl, nz - dz, nz)], pt_r.at[dz, d])
        raised = raised + partin_ref[d - 1]
    raised = raised.reshape(rows, 128)
    hidden = (raised / (1.0 + jnp.exp(-raised))).astype(BF)

    def hpiece(g_, o_, z_):
        return hg_ref.at[g_, o_, :, pl.ds(pl.multiple_of(z_ * 128, 128), 128)]

    def g_from(dz):
        return lambda d: hpiece(add(g, d), o, add(zl, nz - dz, nz))

    def lower(g_, o_):
        r_ = rid(g_, o_, c)
        w = wd_ref[pl.ds(pl.multiple_of(r_ * (nz * 128), 128), nz * 128), :]
        acc_ref[...] += dot(hg_ref[g_, o_], w)

    hg_ref[g, o, :, pl.ds(pl.multiple_of(zl * 128, 128), 128)] = hidden
    own = hpiece(g, o, zl)
    for d in range(1, nz):
        send(own, own, hz_s.at[d], hz_r.at[d], dev(req, add(zl, d, nz), ex))
    spread(own, at_group, hg_s.at[0], hg_r.at[0])
    spread(own, at_other, ho_s.at[0, 0], ho_r.at[0, 0])
    acc_ref[...] = jnp.zeros_like(acc_ref)
    for dz in range(1, nz):
        piece = g_from(dz)(0)
        arrived(piece, hz_r.at[dz])
        spread(piece, at_group, hg_s.at[dz], hg_r.at[dz])
        spread(piece, at_other, ho_s.at[dz, 0], ho_r.at[dz, 0])
    for dz in range(nz):
        for dg in hops:
            piece = g_from(dz)(n - dg)
            arrived(piece, hg_r.at[dz, dg])
            spread(piece, at_other, ho_s.at[dz, dg], ho_r.at[dz, dg])
    for dg in range(n):
        lower(add(g, n - dg), o)
    for dg in (0,) + hops:
        gs = add(g, n - dg)
        for d in hops:
            os = add(o, n - d)
            for dz in range(nz):
                arrived(hpiece(gs, os, add(zl, nz - dz, nz)), ho_r.at[dz, dg, d])
            lower(gs, os)

    ro = iota((plane * nz * 8, rows), 0)
    co = iota((plane * nz * 8, rows), 1)
    low = ro % 8
    zt = (ro // 8) % nz
    spot_of = ro // (8 * nz)
    match = co - low % 2 == (((spot_of // n) * nz + zt) * n + spot_of % n) * 2
    picked = jnp.zeros((plane * nz * 8, 128), F32)
    for k in range(3):
        take = onehot(jnp.logical_and(match, low // 2 == k))
        picked = picked + dot(take, acc_ref[:, k * 128:(k + 1) * 128].astype(BF))
    r1s_ref[...] = picked.reshape(plane, nz, 8, 128).astype(BF)
    spot = o * n + g

    def r1_send(d, carry):
        i = add(spot, d, plane)
        remote(
            r1s_ref.at[i], r1r_ref.at[:, req], r1_s.at[0], r1_r.at[0],
            dev(rid(i % n, i // n, c), zl, ex),
        ).start()
        return carry

    lax.fori_loop(1, plane, r1_send, 0)
    keep = pltpu.make_async_copy(r1s_ref.at[spot], r1r_ref.at[:, req], loc_sem.at[6])
    keep.start()

    rw = iota((g2 * mr, 128), 0)
    low = rw % 8
    expert = jnp.where(low < 6, (rw // mr) * 3 + low // 2 + 1, -1)
    padded = ids_pad[...].astype(I32)
    weights = wt_ref[...]
    ids_pad[0:3, 0:toks] = weights
    weights = ids_pad[...]
    named = jnp.zeros((g2 * mr, 128), F32)
    weight = jnp.zeros((g2 * mr, 128), F32)
    for kk in range(3):
        hit = padded[kk:kk + 1, :] == expert
        named = named + jnp.where(hit, 1.0, 0.0)
        weight = weight + jnp.where(hit, weights[kk:kk + 1, :], 0.0)
    before = dot(named.astype(BF), onehot(r128 < c128))
    comb = jnp.where(before == (rw % 2).astype(F32), weight, 0.0)
    both = [jnp.where((rw % mr) // 8 == i, comb, 0.0).T[0:16] for i in range(hn)]
    both = jnp.concatenate(both, axis=0)
    p0 = both.astype(BF).astype(F32)
    p1 = (both - p0).astype(BF).astype(F32)
    parts = jnp.concatenate([p0, p1, both - p0 - p1], axis=0).astype(BF)

    keep.wait()
    arrived(r1s_ref.at[pl.ds(0, plane - 1)], r1_r.at[0])
    spot2 = zl * g2 + ex

    def r2_src(i):
        e2 = i % g2
        return r1r_ref.at[i // g2, pl.ds((e2 // 2) * n + (e2 % 2) * hn, hn)]

    def r2_send(d, carry):
        i = add(spot2, d, column)
        remote(
            r2_src(i), r2r_ref.at[spot2], r2_s.at[0], r2_r.at[0], dev(req, i // g2, i % g2)
        ).start()
        return carry

    lax.fori_loop(1, column, r2_send, 0)
    keep = pltpu.make_async_copy(r2_src(spot2), r2r_ref.at[spot2], loc_sem.at[7])
    keep.start()
    keep.wait()
    arrived(r2r_ref.at[pl.ds(0, column - 1)], r2_r.at[0])

    sums = [dot(parts, r2r_ref[z * g2:(z + 1) * g2].astype(F32).reshape(g2 * mr, 128).astype(BF)) for z in range(nz)]
    sums = jnp.concatenate(sums, axis=1)
    sums = sums[0:16 * hn] + (sums[16 * hn:32 * hn] + sums[32 * hn:48 * hn])
    pieces = []
    for i in range(hn):
        for z in range(nz):
            pieces.append(sums[i * 16:i * 16 + toks, z * 128:z * 128 + dn])
    total = jnp.concatenate(pieces, axis=1)
    out_ref[...] = (x_ref[...].astype(F32) + total).astype(BF)

    for cp in sends:
        cp.wait_send()

    @pl.when(jnp.logical_not(home))
    def _():
        first.wait_send()
    arrived(r1s_ref.at[pl.ds(0, plane - 1)], r1_s.at[0])
    arrived(r2r_ref.at[pl.ds(0, column - 1)], r2_s.at[0])


def shards(moe_input, route_ids, route_weight, w_up, w_down, queries, keys, values):
    nz = lax.axis_size("head")
    n = math.isqrt(lax.axis_size("req"))
    toks, width = moe_input.shape
    fs = w_up.shape[1]
    dn = w_down.shape[2]
    ffh = w_down.shape[1]
    heads, hd = queries.shape[1:]
    length = keys.shape[1]
    dq = 2 * width
    rows = 2 * n * n * nz
    plane = n * n
    vm = pl.BlockSpec(memory_space=pltpu.VMEM)
    hbm = pl.BlockSpec(memory_space=pl.ANY)
    dma = pltpu.SemaphoreType.DMA
    moe, ctx = pl.pallas_call(
        functools.partial(kernel, n, nz),
        out_shape=(
            jax.ShapeDtypeStruct((toks, width), BF),
            jax.ShapeDtypeStruct((heads, hd), BF),
        ),
        in_specs=[vm, vm, hbm, hbm, hbm, hbm, hbm, hbm],
        out_specs=(vm, vm),
        scratch_shapes=[
            pltpu.VMEM((toks, width), BF),
            pltpu.VMEM((heads, hd), BF),
            pltpu.VMEM((length, hd), BF),
            pltpu.VMEM((length, hd), BF),
            pltpu.VMEM((3, dn, ffh), BF),
            pltpu.VMEM((n, 3, fs, dq), BF),
            pltpu.VMEM((n, 256, width), BF),
            pltpu.VMEM((n * n * nz * 128, 384), BF),
            pltpu.VMEM((128, 128), BF),
            pltpu.VMEM((128, 128), F32),
            pltpu.VMEM((96 * n, 128), BF),
            pltpu.VMEM((96 * n, 128), BF),
            pltpu.VMEM((n, nz, 12 * n, width), BF),
            pltpu.VMEM((n, n, nz, 2 * n, 128), F32),
            pltpu.VMEM((n - 1, n, nz, 2 * n, 128), F32),
            pltpu.VMEM((n, n, rows, nz * 128), BF),
            pltpu.VMEM((rows, 384), F32),
            pltpu.VMEM((plane, nz, 8, 128), BF),
            pltpu.VMEM((nz, plane, 8, 128), BF),
            pltpu.VMEM((2 * n * nz, n // 2, 8, 128), BF),
            dma((8,)),
            dma((n,)), dma((n,)),
            dma((2 * n,)), dma((2 * n,)),
            dma((nz,)), dma((nz,)),
            dma((nz, n)), dma((nz, n)),
            dma((nz, n)), dma((nz, n)),
            dma((nz,)), dma((nz,)),
            dma((nz, n)), dma((nz, n)),
            dma((nz, n, n)), dma((nz, n, n)),
            dma((1,)), dma((1,)),
            dma((1,)), dma((1,)),
        ],
        compiler_params=pltpu.CompilerParams(
            collective_id=0, has_side_effects=True, vmem_limit_bytes=60 * 1024 * 1024
        ),
        cost_estimate=pl.CostEstimate(flops=10**9, bytes_accessed=10**7, transcendentals=10**5),
        name="decode",
    )(
        route_ids.T, route_weight.T, moe_input, queries[0], keys[0], values[0], w_up,
        jnp.swapaxes(w_down, 1, 2),
    )
    return (moe, ctx[None])


def solution(mesh):
    placed = (
        P(("req", "head"), "exp"),
        P(("req", "head"), None),
        P(("req", "head"), None),
        P("exp", ("req", "head"), None),
        P("exp", None, ("req", "head")),
        P(("req", "head", "exp"), None, None),
        P(("req", "head", "exp"), None, None),
        P(("req", "head", "exp"), None, None),
    )
    return jax.shard_map(
        shards,
        mesh=mesh,
        in_specs=placed,
        out_specs=(P(("req", "head"), "exp"), P(("req", "head", "exp"), None, None)),
        check_vma=False,
    )
```

```python
import functools
import math

import jax
import jax.numpy as jnp
from jax import lax
from jax.experimental import pallas as pl
from jax.experimental.pallas import tpu as pltpu
from jax.sharding import PartitionSpec as P

BF = jnp.bfloat16
F32 = jnp.float32
I32 = jnp.int32
NT = (((1,), (1,)), ((), ()))


def iota(shape, dim):
    return lax.broadcasted_iota(I32, shape, dim)


def onehot(match):
    return jnp.where(match, 1.0, 0.0).astype(BF)


def dot(a, b):
    return jnp.dot(a, b, preferred_element_type=F32)


def attend(q, k, v):
    scores = lax.dot_general(q, k, NT, preferred_element_type=F32) * (1.0 / math.sqrt(q.shape[1]))
    weights = jnp.exp(scores - jnp.max(scores, axis=1, keepdims=True))
    total = jnp.sum(weights, axis=1, keepdims=True)
    return (dot(weights.astype(BF), v) / total).astype(BF)


def kernel(
    n, nz,
    ids_ref, wt_ref, x_hbm, q_hbm, k_hbm, v_hbm, up_hbm, down_hbm,
    out_ref, ctx_ref,
    x_ref, q_ref, k_ref, v_ref, down_ref, up_ref, upcat_ref, wt_own, wd_ref,
    tok_ref, ids_pad, send1_ref, recv1_ref, xg_ref, part_ref, partin_ref,
    hg_ref, acc_ref, r1s_ref, r1r_ref, r2s_ref, r2r_ref,
    loc_sem, up_s, up_r, s1_s, s1_r, s2_s, s2_r, s3_s, s3_r,
    pt_s, pt_r, wd_s, wd_r, hz_s, hz_r, ho_s, ho_r,
    r1_s, r1_r, r2_s, r2_r,
):
    toks, width = x_ref.shape
    dq = 2 * width
    chunks = width // 128
    fs = up_ref.shape[2]
    dn = down_ref.shape[1]
    g2 = 2 * n
    unit = 12 * n
    rows = 2 * n * n * nz
    plane = n * n
    column = g2 * nz
    srcs = plane * nz
    hops = (2, 1, 3) if n == 4 else (1,)

    req, zl, ex = lax.axis_index("req"), lax.axis_index("head"), lax.axis_index("exp")
    y, x = req // n, req % n
    zh, c = ex // 2, ex % 2
    g = x * (1 - c) + y * c
    o = y * (1 - c) + x * c

    def rid(g_, o_, c_):
        return (o_ * (1 - c_) + g_ * c_) * n + g_ * (1 - c_) + o_ * c_

    def dev(r_, zl_, ex_):
        return {"req": r_, "head": zl_, "exp": ex_}

    def remote(src, dst, ss, rs, where):
        return pltpu.make_async_remote_copy(
            src_ref=src, dst_ref=dst, send_sem=ss, recv_sem=rs,
            device_id=where, device_id_type=pl.DeviceIdType.MESH,
        )

    def arrived(ref, sem):
        pltpu.make_async_copy(ref, ref, sem).wait()

    def add(v, d, m=n):
        return (v + d) % m

    sends = []

    def send(src, dst, ss, rs, where):
        cp = remote(src, dst, ss, rs, where)
        cp.start()
        sends.append(cp)

    def at_group(d):
        return dev(rid(add(g, d), o, c), zl, ex)

    def at_other(d):
        return dev(rid(g, add(o, d), c), zl, ex)

    def spread(block, where, ss, rs):
        for d in hops:
            send(block, block, ss.at[d], rs.at[d], where(d))

    loads = [
        (x_hbm, x_ref), (q_hbm, q_ref), (k_hbm, k_ref), (v_hbm, v_ref),
        (up_hbm.at[:, :, pl.ds(g * dq, dq)], up_ref.at[g]), (down_hbm, down_ref),
    ]
    loads = [pltpu.make_async_copy(a, b, loc_sem.at[i]) for i, (a, b) in enumerate(loads)]
    for cp in loads:
        cp.start()
    load_x, load_q, load_k, load_v, load_up, load_down = loads

    barrier = pltpu.get_barrier_semaphore()

    def greet(where):
        pl.semaphore_signal(barrier, inc=1, device_id=where, device_id_type=pl.DeviceIdType.MESH)

    def greet_plane(d, carry):
        greet(dev(add(req, d, plane), zl, ex))
        return carry

    def greet_column(d, carry):
        m = add(zl * g2 + ex, d, column)
        greet(dev(req, m // g2, m % g2))
        return carry

    lax.fori_loop(1, column, greet_column, 0)
    lax.fori_loop(1, plane, greet_plane, 0)

    targets = []
    for dz in hops + (0,):
        for dt in range(2):
            t = (c + dt) % 2
            g_t = x * (1 - t) + y * t
            o_t = y * (1 - t) + x * t
            zt = add(zh, dz)
            targets.append((t, g_t, zt, dev(rid(zh, o_t, t), zl, zt * 2 + t), dt == 0 and dz == 0))
    home = g == zh
    for t, g_t, zt, where, own in targets:
        if own:
            @pl.when(jnp.logical_not(home))
            def _():
                greet(where)
        else:
            greet(where)
    for dt in range(2):
        cs = (c + dt) % 2
        for dg in range(n):
            gs = add(g, dg)
            where = dev(rid(gs, o, c), zl, g * 2 + cs)
            if dt == 0 and dg == 0:
                @pl.when(jnp.logical_not(home))
                def _():
                    greet(where)
            else:
                greet(where)

    ids_pad[...] = jnp.zeros_like(ids_pad)
    ids_pad[0:3, 0:toks] = (ids_ref[...] + 1).astype(F32)
    hn = n // 2
    mr = hn * 8
    r128, c128 = iota((128, 128), 0), iota((128, 128), 1)
    tile = onehot(jnp.logical_and(c128 % 16 == r128, r128 < 16))
    tiled = dot(ids_pad[...].astype(BF), tile).astype(I32)
    tri = onehot(jnp.logical_and(r128 // 16 == c128 // 16, r128 % 16 < c128 % 16))
    grp = lax.broadcasted_iota(I32, (g2, 48, 128), 0)
    sub = lax.broadcasted_iota(I32, (g2, 48, 128), 1)
    lane = lax.broadcasted_iota(I32, (g2, 48, 128), 2)
    here = (lane // 16 == sub % 8).reshape(g2 * 48, 128)
    expert = (grp * 3 + sub // 16 + 1).reshape(g2 * 48, 128)
    slot = ((sub // 8) % 2).astype(F32).reshape(g2 * 48, 128)
    named = jnp.zeros((g2 * 48, 128), F32)
    for kk in range(3):
        hit = jnp.logical_and(here, tiled[kk:kk + 1, :] == expert)
        named = named + jnp.where(hit, 1.0, 0.0)
    before = dot(named.astype(BF), tri)
    pick = jnp.where(before == slot, named, 0.0).astype(BF)
    tok_ref[...] = jnp.zeros_like(tok_ref)
    load_x.wait()
    for ch in range(chunks):
        tok_ref[ch * 16:ch * 16 + toks, :] = x_ref[:, ch * 128:(ch + 1) * 128]
    send1_ref[...] = dot(pick, tok_ref[...]).astype(BF)

    @pl.when(home)
    def _():
        pl.semaphore_wait(barrier, plane - 1 + column - 1 + 2 * (2 * n - 1))

    @pl.when(jnp.logical_not(home))
    def _():
        pl.semaphore_wait(barrier, plane - 1 + column - 1 + 2 * (2 * n))

    first = None
    for at, (t, g_t, zt, where, own) in enumerate(targets):
        src = send1_ref.at[pl.ds((zt * 2 + t) * 48, 48), :]
        place = c * n + g_t
        dst = recv1_ref.at[pl.ds(place * 48, 48), :]
        cp = remote(src, dst, s1_s.at[at], s1_r.at[place], where)
        if own:
            first = cp

            @pl.when(home)
            def _():
                pltpu.make_async_copy(src, dst, s1_r.at[place]).start()

            @pl.when(jnp.logical_not(home))
            def _():
                cp.start()
        else:
            cp.start()
            sends.append(cp)

    for d in hops:
        send(
            up_hbm.at[:, :, pl.ds(add(g, d) * dq, dq)], up_ref.at[g],
            up_s.at[d], up_r.at[d], at_group(d),
        )

    load_q.wait()
    load_k.wait()
    load_v.wait()
    ctx_ref[...] = attend(q_ref[...], k_ref[...], v_ref[...])

    batch = min(16, srcs)

    def spread_down(i):
        t = [down_ref[k, :, i * batch * fs:(i + 1) * batch * fs].astype(F32).T for k in range(3)]
        for s in range(batch):
            parts = [t[k][s * fs:(s + 1) * fs] for k in range(3)]
            parts.append(jnp.zeros((128 - 3 * fs, dn), F32))
            at = i * batch + s
            xs, ys = (at // nz) % n, at // nz // n
            gs, os = xs * (1 - c) + ys * c, ys * (1 - c) + xs * c
            row = pl.multiple_of((os * nz + at % nz) * 128, 128)
            wt_own[gs, pl.ds(row, 128), 0:dn] = jnp.concatenate(parts, axis=0).astype(BF)

    load_down.wait()
    wt_own[...] = jnp.zeros_like(wt_own)
    for i in range(srcs // batch):
        spread_down(i)

    def wd_part(g_):
        return wd_ref.at[:, pl.ds(pl.multiple_of(g_ * 128, 128), 128)]

    for d in hops:
        p = add(g, d)
        send(wt_own.at[p], wd_part(g), wd_s.at[d], wd_r.at[d], at_group(d))
    keep_wd = pltpu.make_async_copy(wt_own.at[g], wd_part(g), loc_sem.at[8])
    keep_wd.start()

    ru = lax.broadcasted_iota(I32, (chunks, unit, g2 * 48), 1)
    ch = lax.broadcasted_iota(I32, (chunks, unit, g2 * 48), 0)
    col = lax.broadcasted_iota(I32, (chunks, unit, g2 * 48), 2)
    second = jnp.where(ru >= 6 * n, 1, 0)
    rest = ru - 6 * n * second
    origin = (second * n + (rest % g2) // 2) * 48 + (rest // g2) * 16 + (rest % 2) * 8 + ch
    order = onehot(col == origin).reshape(chunks * unit, g2 * 48)
    for i in range(g2):
        arrived(recv1_ref.at[pl.ds(i * 48, 48), :], s1_r.at[i])
    placed = dot(order, recv1_ref[...]).astype(BF)
    for ch in range(chunks):
        xg_ref[o, zl, :, ch * 128:(ch + 1) * 128] = placed[ch * unit:(ch + 1) * unit]

    own = xg_ref.at[o, zl]
    for d in range(1, nz):
        send(own, own, s2_s.at[d], s2_r.at[d], dev(req, add(zl, d, nz), ex))

    def x_from(dz):
        return lambda d: xg_ref.at[add(o, d), add(zl, nz - dz, nz)]

    spread(own, at_other, s3_s.at[0], s3_r.at[0])
    for dz in range(1, nz):
        block = x_from(dz)(0)
        arrived(block, s2_r.at[dz])
        spread(block, at_other, s3_s.at[dz], s3_r.at[dz])

    def fix_up(p):
        for h in range(2):
            parts = [up_ref[p, k, :, h * width:(h + 1) * width].astype(F32) for k in range(3)]
            parts.append(jnp.zeros((128 - 3 * fs, width), F32))
            upcat_ref[p, h * 128:(h + 1) * 128, :] = jnp.concatenate(parts, axis=0).astype(BF)

    load_up.wait()
    fix_up(g)
    for d in hops:
        p = add(g, n - d)
        arrived(up_ref.at[p], up_r.at[d])
        fix_up(p)

    band = iota((1, 1, 128), 2)

    def products(p, zs):
        a = xg_ref[:, zs].reshape(n * unit, width)
        r = lax.dot_general(a, upcat_ref[p], NT, preferred_element_type=F32)
        r = r.reshape(n, unit, 256)
        total = jnp.zeros((n, g2, 128), F32)
        for h in range(2):
            rk = [
                r[:, (3 * h + k) * g2:(3 * h + k + 1) * g2, h * 128:(h + 1) * 128]
                for k in range(3)
            ]
            total = total + jnp.where(band < fs, rk[0], jnp.where(band < 2 * fs, rk[1], rk[2]))
        part_ref[p, :, zs] = total

    for dz in range(nz):
        for d in hops:
            arrived(x_from(dz)(n - d), s3_r.at[dz, d])
        zs = add(zl, nz - dz, nz)
        for d in hops:
            p = add(g, d)
            products(p, zs)
            send(
                part_ref.at[p, :, zs], partin_ref.at[d - 1, :, zs],
                pt_s.at[dz, d], pt_r.at[dz, d], at_group(d),
            )
        products(g, zs)

    rn = iota((rows, rows), 0)
    src = ((rn // (2 * nz * n)) * nz + (rn % (2 * nz)) // 2) * g2 + ((rn // (2 * nz)) % n) * 2 + rn % 2
    order = onehot(iota((rows, rows), 1) == src)
    raised = part_ref[g]
    for d in hops:
        for dz in range(nz):
            arrived(partin_ref.at[d - 1, :, add(zl, nz - dz, nz)], pt_r.at[dz, d])
        raised = raised + partin_ref[d - 1]
    raised = raised.reshape(rows, 128)
    hidden = (raised / (1.0 + jnp.exp(-raised))).astype(BF)

    hidden = dot(order, hidden).astype(BF)

    def hpiece(o_, z_):
        return hg_ref.at[o_, :, pl.ds(pl.multiple_of(z_ * 128, 128), 128)]

    hg_ref[o, :, pl.ds(pl.multiple_of(zl * 128, 128), 128)] = hidden
    own = hpiece(o, zl)
    for d in range(1, nz):
        send(own, own, hz_s.at[d], hz_r.at[d], dev(req, add(zl, d, nz), ex))
    spread(own, at_other, ho_s.at[0], ho_r.at[0])
    acc_ref[...] = jnp.zeros_like(acc_ref)
    for dz in range(1, nz):
        piece = hpiece(o, add(zl, nz - dz, nz))
        arrived(piece, hz_r.at[dz])
        spread(piece, at_other, ho_s.at[dz], ho_r.at[dz])

    unit_of = iota((1, nz * 128), 1) % 128
    masks = [onehot(jnp.logical_and(unit_of >= k * fs, unit_of < (k + 1) * fs)) for k in range(3)]

    def lower(o_):
        h = hg_ref[o_]
        w = wd_ref[pl.ds(pl.multiple_of(o_ * (nz * 128), 128), nz * 128), :]
        for k in range(3):
            acc_ref[k] += dot(h * masks[k], w)

    keep_wd.wait()
    for d in hops:
        arrived(wd_part(add(g, n - d)), wd_r.at[d])
    lower(o)
    for d in (1, 3, 2) if n == 4 else hops:
        os = add(o, n - d)
        for dz in range(nz):
            arrived(hpiece(os, add(zl, nz - dz, nz)), ho_r.at[dz, d])
        lower(os)

    rz = 2 * nz
    for k in range(3):
        r1s_ref[:, k] = acc_ref[k].reshape(plane, rz, n * 128).astype(BF)
    spot = o * n + g

    def r1_send(d, carry):
        i = add(spot, d, plane)
        remote(
            r1s_ref.at[i], r1r_ref.at[req], r1_s.at[0], r1_r.at[0],
            dev(rid(i % n, i // n, c), zl, ex),
        ).start()
        return carry

    lax.fori_loop(1, plane, r1_send, 0)
    keep = pltpu.make_async_copy(r1s_ref.at[spot], r1r_ref.at[req], loc_sem.at[6])
    keep.start()

    ro = iota((nz * 8, 32), 0)
    low = ro % 8
    order = onehot(jnp.logical_and(
        iota((nz * 8, 32), 1) == (low // 2) * rz + (ro // 8) * 2 + low % 2, low < 6))

    rw = iota((g2 * mr, 128), 0)
    low = rw % 8
    expert = jnp.where(low < 6, (rw // mr) * 3 + low // 2 + 1, -1)
    padded = ids_pad[...].astype(I32)
    weights = wt_ref[...]
    ids_pad[0:3, 0:toks] = weights
    weights = ids_pad[...]
    named = jnp.zeros((g2 * mr, 128), F32)
    weight = jnp.zeros((g2 * mr, 128), F32)
    for kk in range(3):
        hit = padded[kk:kk + 1, :] == expert
        named = named + jnp.where(hit, 1.0, 0.0)
        weight = weight + jnp.where(hit, weights[kk:kk + 1, :], 0.0)
    before = dot(named.astype(BF), onehot(r128 < c128))
    comb = jnp.where(before == (rw % 2).astype(F32), weight, 0.0)
    both = [jnp.where((rw % mr) // 8 == i, comb, 0.0).T[0:16] for i in range(hn)]
    both = jnp.concatenate(both, axis=0)
    p0 = both.astype(BF).astype(F32)
    p1 = (both - p0).astype(BF).astype(F32)
    parts = jnp.concatenate([p0, p1, both - p0 - p1], axis=0).astype(BF)

    keep.wait()
    arrived(r1s_ref.at[pl.ds(0, plane - 1)], r1_r.at[0])
    for os in range(n):
        whole = r1r_ref[rid(0, os, c)].astype(F32)
        for gs in range(1, n):
            whole = whole + r1r_ref[rid(gs, os, c)].astype(F32)
        whole = whole.reshape(3 * rz, n * 128)
        if rz < 8:
            whole = jnp.concatenate([whole, jnp.zeros((32 - 3 * rz, n * 128), F32)], axis=0)
        else:
            whole = jnp.concatenate([whole, jnp.zeros((8, n * 128), F32)], axis=0)
        whole = dot(order, whole.astype(BF))
        for gd in range(n):
            r2s_ref[:, rid(gd, os, c)] = whole[:, gd * 128:(gd + 1) * 128].reshape(nz, 8, 128).astype(BF)
    spot2 = zl * g2 + ex

    def r2_src(i):
        e2 = i % g2
        return r2s_ref.at[i // g2, pl.ds((e2 // 2) * n + (e2 % 2) * hn, hn)]

    def r2_send(d, carry):
        i = add(spot2, d, column)
        remote(
            r2_src(i), r2r_ref.at[spot2], r2_s.at[0], r2_r.at[0], dev(req, i // g2, i % g2)
        ).start()
        return carry

    lax.fori_loop(1, column, r2_send, 0)
    keep = pltpu.make_async_copy(r2_src(spot2), r2r_ref.at[spot2], loc_sem.at[7])
    keep.start()
    keep.wait()
    arrived(r2r_ref.at[pl.ds(0, column - 1)], r2_r.at[0])

    sums = [dot(parts, r2r_ref[z * g2:(z + 1) * g2].astype(F32).reshape(g2 * mr, 128).astype(BF)) for z in range(nz)]
    sums = jnp.concatenate(sums, axis=1)
    sums = sums[0:16 * hn] + (sums[16 * hn:32 * hn] + sums[32 * hn:48 * hn])
    pieces = []
    for i in range(hn):
        for z in range(nz):
            pieces.append(sums[i * 16:i * 16 + toks, z * 128:z * 128 + dn])
    total = jnp.concatenate(pieces, axis=1)
    out_ref[...] = (x_ref[...].astype(F32) + total).astype(BF)

    for cp in sends:
        cp.wait_send()

    @pl.when(jnp.logical_not(home))
    def _():
        first.wait_send()
    arrived(r1s_ref.at[pl.ds(0, plane - 1)], r1_s.at[0])
    arrived(r2r_ref.at[pl.ds(0, column - 1)], r2_s.at[0])


def shards(moe_input, route_ids, route_weight, w_up, w_down, queries, keys, values):
    nz = lax.axis_size("head")
    n = math.isqrt(lax.axis_size("req"))
    toks, width = moe_input.shape
    fs = w_up.shape[1]
    dn = w_down.shape[2]
    ffh = w_down.shape[1]
    heads, hd = queries.shape[1:]
    length = keys.shape[1]
    dq = 2 * width
    rows = 2 * n * n * nz
    plane = n * n
    vm = pl.BlockSpec(memory_space=pltpu.VMEM)
    hbm = pl.BlockSpec(memory_space=pl.ANY)
    dma = pltpu.SemaphoreType.DMA
    moe, ctx = pl.pallas_call(
        functools.partial(kernel, n, nz),
        out_shape=(
            jax.ShapeDtypeStruct((toks, width), BF),
            jax.ShapeDtypeStruct((heads, hd), BF),
        ),
        in_specs=[vm, vm, hbm, hbm, hbm, hbm, hbm, hbm],
        out_specs=(vm, vm),
        scratch_shapes=[
            pltpu.VMEM((toks, width), BF),
            pltpu.VMEM((heads, hd), BF),
            pltpu.VMEM((length, hd), BF),
            pltpu.VMEM((length, hd), BF),
            pltpu.VMEM((3, dn, ffh), BF),
            pltpu.VMEM((n, 3, fs, dq), BF),
            pltpu.VMEM((n, 256, width), BF),
            pltpu.VMEM((n, n * nz * 128, 128), BF),
            pltpu.VMEM((n * nz * 128, n * 128), BF),
            pltpu.VMEM((128, 128), BF),
            pltpu.VMEM((128, 128), F32),
            pltpu.VMEM((96 * n, 128), BF),
            pltpu.VMEM((96 * n, 128), BF),
            pltpu.VMEM((n, nz, 12 * n, width), BF),
            pltpu.VMEM((n, n, nz, 2 * n, 128), F32),
            pltpu.VMEM((n - 1, n, nz, 2 * n, 128), F32),
            pltpu.VMEM((n, rows, nz * 128), BF),
            pltpu.VMEM((3, rows, n * 128), F32),
            pltpu.VMEM((plane, 3, 2 * nz, n * 128), BF),
            pltpu.VMEM((plane, 3, 2 * nz, n * 128), BF),
            pltpu.VMEM((nz, plane, 8, 128), BF),
            pltpu.VMEM((2 * n * nz, n // 2, 8, 128), BF),
            dma((9,)),
            dma((n,)), dma((n,)),
            dma((2 * n,)), dma((2 * n,)),
            dma((nz,)), dma((nz,)),
            dma((nz, n)), dma((nz, n)),
            dma((nz, n)), dma((nz, n)),
            dma((n,)), dma((n,)),
            dma((nz,)), dma((nz,)),
            dma((nz, n)), dma((nz, n)),
            dma((1,)), dma((1,)),
            dma((1,)), dma((1,)),
        ],
        compiler_params=pltpu.CompilerParams(
            collective_id=0, has_side_effects=True, vmem_limit_bytes=55 * 1024 * 1024
        ),
        cost_estimate=pl.CostEstimate(flops=10**9, bytes_accessed=10**7, transcendentals=10**5),
        name="decode",
    )(
        route_ids.T, route_weight.T, moe_input, queries[0], keys[0], values[0], w_up,
        jnp.swapaxes(w_down, 1, 2),
    )
    return (moe, ctx[None])


def solution(mesh):
    placed = (
        P(("req", "head"), "exp"),
        P(("req", "head"), None),
        P(("req", "head"), None),
        P("exp", ("req", "head"), None),
        P("exp", None, ("req", "head")),
        P(("req", "head", "exp"), None, None),
        P(("req", "head", "exp"), None, None),
        P(("req", "head", "exp"), None, None),
    )
    return jax.shard_map(
        shards,
        mesh=mesh,
        in_specs=placed,
        out_specs=(P(("req", "head"), "exp"), P(("req", "head", "exp"), None, None)),
        check_vma=False,
    )
```

```python
import functools
import math

import jax
import jax.numpy as jnp
from jax import lax
from jax.experimental import pallas as pl
from jax.experimental.pallas import tpu as pltpu
from jax.sharding import PartitionSpec as P

BF = jnp.bfloat16
F32 = jnp.float32
I32 = jnp.int32
NT = (((1,), (1,)), ((), ()))


def iota(shape, dim):
    return lax.broadcasted_iota(I32, shape, dim)


def onehot(match):
    return jnp.where(match, 1.0, 0.0).astype(BF)


def dot(a, b):
    return jnp.dot(a, b, preferred_element_type=F32)


def attend(q, k, v):
    scores = lax.dot_general(q, k, NT, preferred_element_type=F32) * (1.0 / math.sqrt(q.shape[1]))
    weights = jnp.exp(scores - jnp.max(scores, axis=1, keepdims=True))
    total = jnp.sum(weights, axis=1, keepdims=True)
    return (dot(weights.astype(BF), v) / total).astype(BF)


def kernel(
    n, nz,
    ids_ref, wt_ref, x_hbm, q_hbm, k_hbm, v_hbm, up_hbm, down_hbm,
    out_ref, ctx_ref,
    x_ref, q_ref, k_ref, v_ref, down_ref, up_ref, upcat_ref, wt_own, wd_ref,
    tok_ref, ids_pad, send1_ref, recv1_ref, xg_ref, part_ref, partin_ref,
    hg_ref, acc_ref, r1s_ref, r1r_ref, r2s_ref, r2r_ref,
    loc_sem, up_s, up_r, s1_s, s1_r, s2_s, s2_r, s3_s, s3_r,
    pt_s, pt_r, wd_s, wd_r, hz_s, hz_r, ho_s, ho_r,
    r1_s, r1_r, r2_s, r2_r,
):
    toks, width = x_ref.shape
    dq = 2 * width
    chunks = width // 128
    fs = up_ref.shape[2]
    dn = down_ref.shape[1]
    g2 = 2 * n
    unit = 12 * n
    rows = 2 * n * n * nz
    plane = n * n
    column = g2 * nz
    srcs = plane * nz
    hops = (2, 1, 3) if n == 4 else (1,)

    req, zl, ex = lax.axis_index("req"), lax.axis_index("head"), lax.axis_index("exp")
    y, x = req // n, req % n
    zh, c = ex // 2, ex % 2
    g = x * (1 - c) + y * c
    o = y * (1 - c) + x * c

    def rid(g_, o_, c_):
        return (o_ * (1 - c_) + g_ * c_) * n + g_ * (1 - c_) + o_ * c_

    def dev(r_, zl_, ex_):
        return {"req": r_, "head": zl_, "exp": ex_}

    def turned(z, f):
        return z + f * (1 - 2 * (z % 2)) if nz > 1 else z

    def remote(src, dst, ss, rs, where):
        return pltpu.make_async_remote_copy(
            src_ref=src, dst_ref=dst, send_sem=ss, recv_sem=rs,
            device_id=where, device_id_type=pl.DeviceIdType.MESH,
        )

    def arrived(ref, sem):
        pltpu.make_async_copy(ref, ref, sem).wait()

    def add(v, d, m=n):
        return (v + d) % m

    away = (zh - g + n) % n
    odd = (away // 2) * (1 - away % 2) if n == 4 else away

    sends = []

    def send(src, dst, ss, rs, where):
        cp = remote(src, dst, ss, rs, where)
        cp.start()
        sends.append(cp)

    def at_group(d):
        return dev(rid(add(g, d), o, c), zl, ex)

    def at_other(d):
        return dev(rid(g, add(o, d), c), zl, ex)

    def spread(block, where, ss, rs):
        for d in hops:
            send(block, block, ss.at[d], rs.at[d], where(d))

    loads = [
        (x_hbm, x_ref), (q_hbm, q_ref), (k_hbm, k_ref), (v_hbm, v_ref),
        (up_hbm.at[:, :, pl.ds(g * dq, dq)], up_ref.at[g]), (down_hbm, down_ref),
    ]
    loads = [pltpu.make_async_copy(a, b, loc_sem.at[i]) for i, (a, b) in enumerate(loads)]
    for cp in loads:
        cp.start()
    load_x, load_q, load_k, load_v, load_up, load_down = loads

    barrier = pltpu.get_barrier_semaphore()

    def greet(where):
        pl.semaphore_signal(barrier, inc=1, device_id=where, device_id_type=pl.DeviceIdType.MESH)

    def greet_plane(d, carry):
        greet(dev(add(req, d, plane), zl, ex))
        return carry

    def greet_column(d, carry):
        m = add(zl * g2 + ex, d, column)
        greet(dev(req, m // g2, m % g2))
        return carry

    targets = []
    for dz in hops + (0,):
        for dt in range(2):
            t = (c + dt) % 2
            g_t = x * (1 - t) + y * t
            o_t = y * (1 - t) + x * t
            zt = add(zh, dz)
            targets.append((t, g_t, zt, dev(rid(zh, o_t, t), turned(zl, 1 if dz == n // 2 else 0), zt * 2 + t), dt == 0 and dz == 0))
    home = g == zh
    for t, g_t, zt, where, own in targets:
        if own:
            @pl.when(jnp.logical_not(home))
            def _():
                greet(where)
        else:
            greet(where)
    for dt in range(2):
        cs = (c + dt) % 2
        for dg in range(n):
            gs = add(g, dg)
            where = dev(rid(gs, o, c), turned(zl, odd), g * 2 + cs)
            if dt == 0 and dg == 0:
                @pl.when(jnp.logical_not(home))
                def _():
                    greet(where)
            else:
                greet(where)

    lax.fori_loop(1, column, greet_column, 0)
    lax.fori_loop(1, plane, greet_plane, 0)

    ids_pad[...] = jnp.zeros_like(ids_pad)
    ids_pad[0:3, 0:toks] = (ids_ref[...] + 1).astype(F32)
    hn = n // 2
    mr = hn * 8
    r128, c128 = iota((128, 128), 0), iota((128, 128), 1)
    tile = onehot(jnp.logical_and(c128 % 16 == r128, r128 < 16))
    tiled = dot(ids_pad[...].astype(BF), tile).astype(I32)
    tri = onehot(jnp.logical_and(r128 // 16 == c128 // 16, r128 % 16 < c128 % 16))
    grp = lax.broadcasted_iota(I32, (g2, 48, 128), 0)
    sub = lax.broadcasted_iota(I32, (g2, 48, 128), 1)
    lane = lax.broadcasted_iota(I32, (g2, 48, 128), 2)
    here = (lane // 16 == sub % 8).reshape(g2 * 48, 128)
    expert = (grp * 3 + sub // 16 + 1).reshape(g2 * 48, 128)
    slot = ((sub // 8) % 2).astype(F32).reshape(g2 * 48, 128)
    named = jnp.zeros((g2 * 48, 128), F32)
    for kk in range(3):
        hit = jnp.logical_and(here, tiled[kk:kk + 1, :] == expert)
        named = named + jnp.where(hit, 1.0, 0.0)
    before = dot(named.astype(BF), tri)
    pick = jnp.where(before == slot, named, 0.0).astype(BF)
    tok_ref[...] = jnp.zeros_like(tok_ref)
    load_x.wait()
    for ch in range(chunks):
        tok_ref[ch * 16:ch * 16 + toks, :] = x_ref[:, ch * 128:(ch + 1) * 128]
    send1_ref[...] = dot(pick, tok_ref[...]).astype(BF)

    @pl.when(home)
    def _():
        pl.semaphore_wait(barrier, plane - 1 + column - 1 + 2 * (2 * n - 1))

    @pl.when(jnp.logical_not(home))
    def _():
        pl.semaphore_wait(barrier, plane - 1 + column - 1 + 2 * (2 * n))

    first = None
    for at, (t, g_t, zt, where, own) in enumerate(targets):
        src = send1_ref.at[pl.ds((zt * 2 + t) * 48, 48), :]
        place = c * n + g_t
        dst = recv1_ref.at[pl.ds(place * 48, 48), :]
        cp = remote(src, dst, s1_s.at[at], s1_r.at[place], where)
        if own:
            first = cp

            @pl.when(home)
            def _():
                pltpu.make_async_copy(src, dst, s1_r.at[place]).start()

            @pl.when(jnp.logical_not(home))
            def _():
                cp.start()
        else:
            cp.start()
            sends.append(cp)

    for d in hops:
        send(
            up_hbm.at[:, :, pl.ds(add(g, d) * dq, dq)], up_ref.at[g],
            up_s.at[d], up_r.at[d], at_group(d),
        )

    load_q.wait()
    load_k.wait()
    load_v.wait()
    ctx_ref[...] = attend(q_ref[...], k_ref[...], v_ref[...])

    batch = min(16, srcs)

    def spread_down(i):
        t = [down_ref[k, :, i * batch * fs:(i + 1) * batch * fs].astype(F32).T for k in range(3)]
        for s in range(batch):
            parts = [t[k][s * fs:(s + 1) * fs] for k in range(3)]
            parts.append(jnp.zeros((128 - 3 * fs, dn), F32))
            at = i * batch + s
            xs, ys = (at // nz) % n, at // nz // n
            gs, os = xs * (1 - c) + ys * c, ys * (1 - c) + xs * c
            row = pl.multiple_of((os * nz + at % nz) * 128, 128)
            wt_own[gs, pl.ds(row, 128), 0:dn] = jnp.concatenate(parts, axis=0).astype(BF)

    load_down.wait()
    wt_own[...] = jnp.zeros_like(wt_own)
    for i in range(srcs // batch):
        spread_down(i)

    def wd_part(g_):
        return wd_ref.at[:, pl.ds(pl.multiple_of(g_ * 128, 128), 128)]

    def send_wd(d):
        send(wt_own.at[add(g, d)], wd_part(g), wd_s.at[d], wd_r.at[d], at_group(d))

    send_wd(hops[0])
    keep_wd = pltpu.make_async_copy(wt_own.at[g], wd_part(g), loc_sem.at[8])
    keep_wd.start()

    ru = lax.broadcasted_iota(I32, (chunks, unit, g2 * 48), 1)
    ch = lax.broadcasted_iota(I32, (chunks, unit, g2 * 48), 0)
    col = lax.broadcasted_iota(I32, (chunks, unit, g2 * 48), 2)
    second = jnp.where(ru >= 6 * n, 1, 0)
    rest = ru - 6 * n * second
    origin = (second * n + (rest % g2) // 2) * 48 + (rest // g2) * 16 + (rest % 2) * 8 + ch
    order = onehot(col == origin).reshape(chunks * unit, g2 * 48)
    for i in range(g2):
        arrived(recv1_ref.at[pl.ds(i * 48, 48), :], s1_r.at[i])
    placed = dot(order, recv1_ref[...]).astype(BF)
    for ch in range(chunks):
        xg_ref[o, turned(zl, odd), :, ch * 128:(ch + 1) * 128] = placed[ch * unit:(ch + 1) * unit]

    own = xg_ref.at[o, turned(zl, odd)]
    for d in range(1, nz):
        send(own, own, s2_s.at[d], s2_r.at[d], dev(req, add(zl, d, nz), ex))

    def x_from(dz):
        return lambda d: xg_ref.at[add(o, d), turned(add(zl, nz - dz, nz), odd)]

    spread(own, at_other, s3_s.at[0], s3_r.at[0])
    for dz in range(1, nz):
        block = x_from(dz)(0)
        arrived(block, s2_r.at[dz])
        spread(block, at_other, s3_s.at[dz], s3_r.at[dz])

    def fix_up(p):
        for h in range(2):
            parts = [up_ref[p, k, :, h * width:(h + 1) * width].astype(F32) for k in range(3)]
            parts.append(jnp.zeros((128 - 3 * fs, width), F32))
            upcat_ref[p, h * 128:(h + 1) * 128, :] = jnp.concatenate(parts, axis=0).astype(BF)

    load_up.wait()
    fix_up(g)
    for d in hops:
        p = add(g, n - d)
        arrived(up_ref.at[p], up_r.at[d])
        fix_up(p)

    band = iota((1, 1, 128), 2)

    def products(p, zs):
        a = xg_ref[:, zs].reshape(n * unit, width)
        r = lax.dot_general(a, upcat_ref[p], NT, preferred_element_type=F32)
        r = r.reshape(n, unit, 256)
        total = jnp.zeros((n, g2, 128), F32)
        for h in range(2):
            rk = [
                r[:, (3 * h + k) * g2:(3 * h + k + 1) * g2, h * 128:(h + 1) * 128]
                for k in range(3)
            ]
            total = total + jnp.where(band < fs, rk[0], jnp.where(band < 2 * fs, rk[1], rk[2]))
        part_ref[p, :, zs] = total

    for dz in range(nz):
        for d in hops:
            arrived(x_from(dz)(n - d), s3_r.at[dz, d])
        zs = turned(add(zl, nz - dz, nz), odd)
        for d in hops:
            p = add(g, d)
            products(p, zs)
            send(
                part_ref.at[p, :, zs], partin_ref.at[d - 1, :, zs],
                pt_s.at[dz, d], pt_r.at[dz, d], at_group(d),
            )
        products(g, zs)

    for d in hops[1:]:
        send_wd(d)

    rn = iota((rows, rows), 0)
    src = ((rn // (2 * nz * n)) * nz + (rn % (2 * nz)) // 2) * g2 + ((rn // (2 * nz)) % n) * 2 + rn % 2
    order = onehot(iota((rows, rows), 1) == src)
    raised = part_ref[g]
    for d in hops:
        for dz in range(nz):
            arrived(partin_ref.at[d - 1, :, add(zl, nz - dz, nz)], pt_r.at[dz, d])
        raised = raised + partin_ref[d - 1]
    raised = raised.reshape(rows, 128)
    hidden = (raised / (1.0 + jnp.exp(-raised))).astype(BF)

    hidden = dot(order, hidden).astype(BF)

    def hpiece(o_, z_):
        return hg_ref.at[o_, :, pl.ds(pl.multiple_of(z_ * 128, 128), 128)]

    hg_ref[o, :, pl.ds(pl.multiple_of(zl * 128, 128), 128)] = hidden
    own = hpiece(o, zl)
    for d in range(1, nz):
        send(own, own, hz_s.at[d], hz_r.at[d], dev(req, add(zl, d, nz), ex))
    spread(own, at_other, ho_s.at[0], ho_r.at[0])
    acc_ref[...] = jnp.zeros_like(acc_ref)
    for dz in range(1, nz):
        piece = hpiece(o, add(zl, nz - dz, nz))
        arrived(piece, hz_r.at[dz])
        spread(piece, at_other, ho_s.at[dz], ho_r.at[dz])

    unit_of = iota((1, nz * 128), 1) % 128
    masks = [onehot(jnp.logical_and(unit_of >= k * fs, unit_of < (k + 1) * fs)) for k in range(3)]

    def lower(o_):
        h = hg_ref[o_]
        w = wd_ref[pl.ds(pl.multiple_of(o_ * (nz * 128), 128), nz * 128), :]
        for k in range(3):
            acc_ref[k] += dot(h * masks[k], w)

    keep_wd.wait()
    for d in hops:
        arrived(wd_part(add(g, n - d)), wd_r.at[d])
    lower(o)
    for d in (1, 3, 2) if n == 4 else hops:
        os = add(o, n - d)
        for dz in range(nz):
            arrived(hpiece(os, add(zl, nz - dz, nz)), ho_r.at[dz, d])
        lower(os)

    rz = 2 * nz
    for k in range(3):
        r1s_ref[:, k] = acc_ref[k].reshape(plane, rz, n * 128).astype(BF)
    spot = o * n + g

    def r1_send(d, carry):
        i = add(spot, d, plane)
        remote(
            r1s_ref.at[i], r1r_ref.at[req], r1_s.at[0], r1_r.at[0],
            dev(rid(i % n, i // n, c), zl, ex),
        ).start()
        return carry

    lax.fori_loop(1, plane, r1_send, 0)
    keep = pltpu.make_async_copy(r1s_ref.at[spot], r1r_ref.at[req], loc_sem.at[6])
    keep.start()

    ro = iota((nz * 8, 32), 0)
    low = ro % 8
    order = onehot(jnp.logical_and(
        iota((nz * 8, 32), 1) == (low // 2) * rz + (ro // 8) * 2 + low % 2, low < 6))

    rw = iota((g2 * mr, 128), 0)
    low = rw % 8
    expert = jnp.where(low < 6, (rw // mr) * 3 + low // 2 + 1, -1)
    padded = ids_pad[...].astype(I32)
    weights = wt_ref[...]
    ids_pad[0:3, 0:toks] = weights
    weights = ids_pad[...]
    named = jnp.zeros((g2 * mr, 128), F32)
    weight = jnp.zeros((g2 * mr, 128), F32)
    for kk in range(3):
        hit = padded[kk:kk + 1, :] == expert
        named = named + jnp.where(hit, 1.0, 0.0)
        weight = weight + jnp.where(hit, weights[kk:kk + 1, :], 0.0)
    before = dot(named.astype(BF), onehot(r128 < c128))
    comb = jnp.where(before == (rw % 2).astype(F32), weight, 0.0)
    both = [jnp.where((rw % mr) // 8 == i, comb, 0.0).T[0:16] for i in range(hn)]
    both = jnp.concatenate(both, axis=0)
    p0 = both.astype(BF).astype(F32)
    p1 = (both - p0).astype(BF).astype(F32)
    parts = jnp.concatenate([p0, p1, both - p0 - p1], axis=0).astype(BF)

    keep.wait()
    arrived(r1s_ref.at[pl.ds(0, plane - 1)], r1_r.at[0])
    for os in range(n):
        whole = r1r_ref[rid(0, os, c)].astype(F32)
        for gs in range(1, n):
            whole = whole + r1r_ref[rid(gs, os, c)].astype(F32)
        whole = whole.reshape(3 * rz, n * 128)
        if rz < 8:
            whole = jnp.concatenate([whole, jnp.zeros((32 - 3 * rz, n * 128), F32)], axis=0)
        else:
            whole = jnp.concatenate([whole, jnp.zeros((8, n * 128), F32)], axis=0)
        whole = dot(order, whole.astype(BF))
        for gd in range(n):
            r2s_ref[:, rid(gd, os, c)] = whole[:, gd * 128:(gd + 1) * 128].reshape(nz, 8, 128).astype(BF)
    spot2 = zl * g2 + ex

    def r2_src(i):
        e2 = i % g2
        return r2s_ref.at[i // g2, pl.ds((e2 // 2) * n + (e2 % 2) * hn, hn)]

    def r2_send(d, carry):
        i = add(spot2, d, column)
        remote(
            r2_src(i), r2r_ref.at[spot2], r2_s.at[0], r2_r.at[0], dev(req, i // g2, i % g2)
        ).start()
        return carry

    lax.fori_loop(1, column, r2_send, 0)
    keep = pltpu.make_async_copy(r2_src(spot2), r2r_ref.at[spot2], loc_sem.at[7])
    keep.start()
    keep.wait()
    arrived(r2r_ref.at[pl.ds(0, column - 1)], r2_r.at[0])

    sums = [dot(parts, r2r_ref[z * g2:(z + 1) * g2].astype(F32).reshape(g2 * mr, 128).astype(BF)) for z in range(nz)]
    sums = jnp.concatenate(sums, axis=1)
    sums = sums[0:16 * hn] + (sums[16 * hn:32 * hn] + sums[32 * hn:48 * hn])
    pieces = []
    for i in range(hn):
        for z in range(nz):
            pieces.append(sums[i * 16:i * 16 + toks, z * 128:z * 128 + dn])
    total = jnp.concatenate(pieces, axis=1)
    out_ref[...] = (x_ref[...].astype(F32) + total).astype(BF)

    for cp in sends:
        cp.wait_send()

    @pl.when(jnp.logical_not(home))
    def _():
        first.wait_send()
    arrived(r1s_ref.at[pl.ds(0, plane - 1)], r1_s.at[0])
    arrived(r2r_ref.at[pl.ds(0, column - 1)], r2_s.at[0])


def shards(moe_input, route_ids, route_weight, w_up, w_down, queries, keys, values):
    nz = lax.axis_size("head")
    n = math.isqrt(lax.axis_size("req"))
    toks, width = moe_input.shape
    fs = w_up.shape[1]
    dn = w_down.shape[2]
    ffh = w_down.shape[1]
    heads, hd = queries.shape[1:]
    length = keys.shape[1]
    dq = 2 * width
    rows = 2 * n * n * nz
    plane = n * n
    vm = pl.BlockSpec(memory_space=pltpu.VMEM)
    hbm = pl.BlockSpec(memory_space=pl.ANY)
    dma = pltpu.SemaphoreType.DMA
    moe, ctx = pl.pallas_call(
        functools.partial(kernel, n, nz),
        out_shape=(
            jax.ShapeDtypeStruct((toks, width), BF),
            jax.ShapeDtypeStruct((heads, hd), BF),
        ),
        in_specs=[vm, vm, hbm, hbm, hbm, hbm, hbm, hbm],
        out_specs=(vm, vm),
        scratch_shapes=[
            pltpu.VMEM((toks, width), BF),
            pltpu.VMEM((heads, hd), BF),
            pltpu.VMEM((length, hd), BF),
            pltpu.VMEM((length, hd), BF),
            pltpu.VMEM((3, dn, ffh), BF),
            pltpu.VMEM((n, 3, fs, dq), BF),
            pltpu.VMEM((n, 256, width), BF),
            pltpu.VMEM((n, n * nz * 128, 128), BF),
            pltpu.VMEM((n * nz * 128, n * 128), BF),
            pltpu.VMEM((128, 128), BF),
            pltpu.VMEM((128, 128), F32),
            pltpu.VMEM((96 * n, 128), BF),
            pltpu.VMEM((96 * n, 128), BF),
            pltpu.VMEM((n, nz, 12 * n, width), BF),
            pltpu.VMEM((n, n, nz, 2 * n, 128), F32),
            pltpu.VMEM((n - 1, n, nz, 2 * n, 128), F32),
            pltpu.VMEM((n, rows, nz * 128), BF),
            pltpu.VMEM((3, rows, n * 128), F32),
            pltpu.VMEM((plane, 3, 2 * nz, n * 128), BF),
            pltpu.VMEM((plane, 3, 2 * nz, n * 128), BF),
            pltpu.VMEM((nz, plane, 8, 128), BF),
            pltpu.VMEM((2 * n * nz, n // 2, 8, 128), BF),
            dma((9,)),
            dma((n,)), dma((n,)),
            dma((2 * n,)), dma((2 * n,)),
            dma((nz,)), dma((nz,)),
            dma((nz, n)), dma((nz, n)),
            dma((nz, n)), dma((nz, n)),
            dma((n,)), dma((n,)),
            dma((nz,)), dma((nz,)),
            dma((nz, n)), dma((nz, n)),
            dma((1,)), dma((1,)),
            dma((1,)), dma((1,)),
        ],
        compiler_params=pltpu.CompilerParams(
            collective_id=0, has_side_effects=True, vmem_limit_bytes=55 * 1024 * 1024
        ),
        cost_estimate=pl.CostEstimate(flops=10**9, bytes_accessed=10**7, transcendentals=10**5),
        name="decode",
    )(
        route_ids.T, route_weight.T, moe_input, queries[0], keys[0], values[0], w_up,
        jnp.swapaxes(w_down, 1, 2),
    )
    return (moe, ctx[None])


def solution(mesh):
    placed = (
        P(("req", "head"), "exp"),
        P(("req", "head"), None),
        P(("req", "head"), None),
        P("exp", ("req", "head"), None),
        P("exp", None, ("req", "head")),
        P(("req", "head", "exp"), None, None),
        P(("req", "head", "exp"), None, None),
        P(("req", "head", "exp"), None, None),
    )
    return jax.shard_map(
        shards,
        mesh=mesh,
        in_specs=placed,
        out_specs=(P(("req", "head"), "exp"), P(("req", "head", "exp"), None, None)),
        check_vma=False,
    )
```

```python
import functools
import math

import jax
import jax.numpy as jnp
from jax import lax
from jax.experimental import pallas as pl
from jax.experimental.pallas import tpu as pltpu
from jax.sharding import PartitionSpec as P

BF = jnp.bfloat16
F32 = jnp.float32
I32 = jnp.int32
NT = (((1,), (1,)), ((), ()))


def iota(shape, dim):
    return lax.broadcasted_iota(I32, shape, dim)


def onehot(match):
    return jnp.where(match, 1.0, 0.0).astype(BF)


def dot(a, b):
    return jnp.dot(a, b, preferred_element_type=F32)


def attend(q, k, v):
    scores = lax.dot_general(q, k, NT, preferred_element_type=F32) * (1.0 / math.sqrt(q.shape[1]))
    weights = jnp.exp(scores - jnp.max(scores, axis=1, keepdims=True))
    total = jnp.sum(weights, axis=1, keepdims=True)
    return (dot(weights.astype(BF), v) / total).astype(BF)


def kernel(
    n, nz,
    ids_ref, wt_ref, x_hbm, q_hbm, k_hbm, v_hbm, up_hbm, down_hbm,
    out_ref, ctx_ref,
    x_ref, q_ref, k_ref, v_ref, down_ref, up_ref, upcat_ref, wt_own, wd_ref,
    tok_ref, ids_pad, send1_ref, recv1_ref, xg_ref, part_ref, partin_ref,
    hg_ref, acc_ref, r1s_ref, r1r_ref, r2s_ref, r2r_ref,
    loc_sem, up_s, up_r, s1_s, s1_r, s2_s, s2_r, s3_s, s3_r,
    pt_s, pt_r, wd_s, wd_r, hz_s, hz_r, ho_s, ho_r,
    r1_s, r1_r, r2_s, r2_r,
):
    toks, width = x_ref.shape
    dq = 2 * width
    chunks = width // 128
    fs = up_ref.shape[2]
    dn = down_ref.shape[1]
    g2 = 2 * n
    unit = 12 * n
    rows = 2 * n * n * nz
    plane = n * n
    column = g2 * nz
    srcs = plane * nz
    hops = (2, 1, 3) if n == 4 else (1,)

    req, zl, ex = lax.axis_index("req"), lax.axis_index("head"), lax.axis_index("exp")
    y, x = req // n, req % n
    zh, c = ex // 2, ex % 2
    g = x * (1 - c) + y * c
    o = y * (1 - c) + x * c

    def rid(g_, o_, c_):
        return (o_ * (1 - c_) + g_ * c_) * n + g_ * (1 - c_) + o_ * c_

    def dev(r_, zl_, ex_):
        return {"req": r_, "head": zl_, "exp": ex_}

    def turned(z, f):
        return z + f * (1 - 2 * (z % 2)) if nz > 1 else z

    def remote(src, dst, ss, rs, where):
        return pltpu.make_async_remote_copy(
            src_ref=src, dst_ref=dst, send_sem=ss, recv_sem=rs,
            device_id=where, device_id_type=pl.DeviceIdType.MESH,
        )

    def arrived(ref, sem):
        pltpu.make_async_copy(ref, ref, sem).wait()

    def add(v, d, m=n):
        return (v + d) % m

    away = (zh - g + n) % n
    odd = (away // 2) * (1 - away % 2) if n == 4 else away

    sends = []

    def send(src, dst, ss, rs, where):
        cp = remote(src, dst, ss, rs, where)
        cp.start()
        sends.append(cp)

    def at_group(d):
        return dev(rid(add(g, d), o, c), zl, ex)

    def at_other(d):
        return dev(rid(g, add(o, d), c), zl, ex)

    def spread(block, where, ss, rs):
        for d in hops:
            send(block, block, ss.at[d], rs.at[d], where(d))

    loads = [
        (x_hbm, x_ref), (q_hbm, q_ref), (k_hbm, k_ref), (v_hbm, v_ref),
        (up_hbm.at[:, :, pl.ds(g * dq, dq)], up_ref.at[g]), (down_hbm, down_ref),
    ]
    loads = [pltpu.make_async_copy(a, b, loc_sem.at[i]) for i, (a, b) in enumerate(loads)]
    for cp in loads:
        cp.start()
    load_x, load_q, load_k, load_v, load_up, load_down = loads

    barrier = pltpu.get_barrier_semaphore()

    def greet(where):
        pl.semaphore_signal(barrier, inc=1, device_id=where, device_id_type=pl.DeviceIdType.MESH)

    def greet_plane(d, carry):
        greet(dev(add(req, d, plane), zl, ex))
        return carry

    def greet_column(d, carry):
        m = add(zl * g2 + ex, d, column)
        greet(dev(req, m // g2, m % g2))
        return carry

    targets = []
    for dz in hops + (0,):
        for dt in range(2):
            t = (c + dt) % 2
            g_t = x * (1 - t) + y * t
            o_t = y * (1 - t) + x * t
            zt = add(zh, dz)
            targets.append((t, g_t, zt, dev(rid(zh, o_t, t), turned(zl, 1 if dz == n // 2 else 0), zt * 2 + t), dt == 0 and dz == 0))
    home = g == zh
    for t, g_t, zt, where, own in targets:
        if own:
            @pl.when(jnp.logical_not(home))
            def _():
                greet(where)
        else:
            greet(where)
    for dt in range(2):
        cs = (c + dt) % 2
        for dg in range(n):
            gs = add(g, dg)
            where = dev(rid(gs, o, c), turned(zl, odd), g * 2 + cs)
            if dt == 0 and dg == 0:
                @pl.when(jnp.logical_not(home))
                def _():
                    greet(where)
            else:
                greet(where)

    lax.fori_loop(1, column, greet_column, 0)
    lax.fori_loop(1, plane, greet_plane, 0)

    ids_pad[...] = jnp.zeros_like(ids_pad)
    ids_pad[0:3, 0:toks] = (ids_ref[...] + 1).astype(F32)
    hn = n // 2
    mr = hn * 8
    r128, c128 = iota((128, 128), 0), iota((128, 128), 1)
    tile = onehot(jnp.logical_and(c128 % 16 == r128, r128 < 16))
    tiled = dot(ids_pad[...].astype(BF), tile).astype(I32)
    tri = onehot(jnp.logical_and(r128 // 16 == c128 // 16, r128 % 16 < c128 % 16))
    grp = lax.broadcasted_iota(I32, (g2, 48, 128), 0)
    sub = lax.broadcasted_iota(I32, (g2, 48, 128), 1)
    lane = lax.broadcasted_iota(I32, (g2, 48, 128), 2)
    here = (lane // 16 == sub % 8).reshape(g2 * 48, 128)
    expert = (grp * 3 + sub // 16 + 1).reshape(g2 * 48, 128)
    slot = ((sub // 8) % 2).astype(F32).reshape(g2 * 48, 128)
    named = jnp.zeros((g2 * 48, 128), F32)
    for kk in range(3):
        hit = jnp.logical_and(here, tiled[kk:kk + 1, :] == expert)
        named = named + jnp.where(hit, 1.0, 0.0)
    before = dot(named.astype(BF), tri)
    pick = jnp.where(before == slot, named, 0.0).astype(BF)
    tok_ref[...] = jnp.zeros_like(tok_ref)
    load_x.wait()
    for ch in range(chunks):
        tok_ref[ch * 16:ch * 16 + toks, :] = x_ref[:, ch * 128:(ch + 1) * 128]
    send1_ref[...] = dot(pick, tok_ref[...]).astype(BF)

    @pl.when(home)
    def _():
        pl.semaphore_wait(barrier, plane - 1 + column - 1 + 2 * (2 * n - 1))

    @pl.when(jnp.logical_not(home))
    def _():
        pl.semaphore_wait(barrier, plane - 1 + column - 1 + 2 * (2 * n))

    first = None
    for at, (t, g_t, zt, where, own) in enumerate(targets):
        src = send1_ref.at[pl.ds((zt * 2 + t) * 48, 48), :]
        place = c * n + g_t
        dst = recv1_ref.at[pl.ds(place * 48, 48), :]
        cp = remote(src, dst, s1_s.at[at], s1_r.at[place], where)
        if own:
            first = cp

            @pl.when(home)
            def _():
                pltpu.make_async_copy(src, dst, s1_r.at[place]).start()

            @pl.when(jnp.logical_not(home))
            def _():
                cp.start()
        else:
            cp.start()
            sends.append(cp)

    for d in hops:
        send(
            up_hbm.at[:, :, pl.ds(add(g, d) * dq, dq)], up_ref.at[g],
            up_s.at[d], up_r.at[d], at_group(d),
        )

    load_q.wait()
    load_k.wait()
    load_v.wait()
    ctx_ref[...] = attend(q_ref[...], k_ref[...], v_ref[...])

    batch = min(16, srcs)

    def spread_down(i):
        t = [down_ref[k, :, i * batch * fs:(i + 1) * batch * fs].astype(F32).T for k in range(3)]
        for s in range(batch):
            parts = [t[k][s * fs:(s + 1) * fs] for k in range(3)]
            parts.append(jnp.zeros((128 - 3 * fs, dn), F32))
            at = i * batch + s
            xs, ys = (at // nz) % n, at // nz // n
            gs, os = xs * (1 - c) + ys * c, ys * (1 - c) + xs * c
            row = pl.multiple_of((os * nz + at % nz) * 128, 128)
            wt_own[gs, pl.ds(row, 128), 0:dn] = jnp.concatenate(parts, axis=0).astype(BF)

    load_down.wait()
    wt_own[...] = jnp.zeros_like(wt_own)
    for i in range(srcs // batch):
        spread_down(i)

    def wd_part(g_):
        return wd_ref.at[:, pl.ds(pl.multiple_of(g_ * 128, 128), 128)]

    def send_wd(d):
        send(wt_own.at[add(g, d)], wd_part(g), wd_s.at[d], wd_r.at[d], at_group(d))

    send_wd(hops[0])
    keep_wd = pltpu.make_async_copy(wt_own.at[g], wd_part(g), loc_sem.at[8])
    keep_wd.start()

    ru = lax.broadcasted_iota(I32, (chunks, unit, g2 * 48), 1)
    ch = lax.broadcasted_iota(I32, (chunks, unit, g2 * 48), 0)
    col = lax.broadcasted_iota(I32, (chunks, unit, g2 * 48), 2)
    second = jnp.where(ru >= 6 * n, 1, 0)
    rest = ru - 6 * n * second
    origin = (second * n + (rest % g2) // 2) * 48 + (rest // g2) * 16 + (rest % 2) * 8 + ch
    order = onehot(col == origin).reshape(chunks * unit, g2 * 48)
    for i in range(g2):
        arrived(recv1_ref.at[pl.ds(i * 48, 48), :], s1_r.at[i])
    placed = dot(order, recv1_ref[...]).astype(BF)
    for ch in range(chunks):
        xg_ref[o, turned(zl, odd), :, ch * 128:(ch + 1) * 128] = placed[ch * unit:(ch + 1) * unit]

    own = xg_ref.at[o, turned(zl, odd)]
    for d in range(1, nz):
        send(own, own, s2_s.at[d], s2_r.at[d], dev(req, add(zl, d, nz), ex))

    def x_from(dz):
        return lambda d: xg_ref.at[add(o, d), turned(add(zl, nz - dz, nz), odd)]

    spread(own, at_other, s3_s.at[0], s3_r.at[0])
    for dz in range(1, nz):
        block = x_from(dz)(0)
        arrived(block, s2_r.at[dz])
        spread(block, at_other, s3_s.at[dz], s3_r.at[dz])

    def fix_up(p):
        for h in range(2):
            parts = [up_ref[p, k, :, h * width:(h + 1) * width].astype(F32) for k in range(3)]
            parts.append(jnp.zeros((128 - 3 * fs, width), F32))
            upcat_ref[p, h * 128:(h + 1) * 128, :] = jnp.concatenate(parts, axis=0).astype(BF)

    load_up.wait()
    fix_up(g)
    for d in hops:
        p = add(g, n - d)
        arrived(up_ref.at[p], up_r.at[d])
        fix_up(p)

    band = iota((1, 1, 128), 2)

    def products(p, zs):
        a = xg_ref[:, zs].reshape(n * unit, width)
        r = lax.dot_general(a, upcat_ref[p], NT, preferred_element_type=F32)
        r = r.reshape(n, unit, 256)
        total = jnp.zeros((n, g2, 128), F32)
        for h in range(2):
            rk = [
                r[:, (3 * h + k) * g2:(3 * h + k + 1) * g2, h * 128:(h + 1) * 128]
                for k in range(3)
            ]
            total = total + jnp.where(band < fs, rk[0], jnp.where(band < 2 * fs, rk[1], rk[2]))
        part_ref[p, :, zs] = total

    for dz in range(nz):
        for d in hops:
            arrived(x_from(dz)(n - d), s3_r.at[dz, d])
        zs = turned(add(zl, nz - dz, nz), odd)
        for d in hops:
            p = add(g, d)
            products(p, zs)
            send(
                part_ref.at[p, :, zs], partin_ref.at[d - 1, :, zs],
                pt_s.at[dz, d], pt_r.at[dz, d], at_group(d),
            )
        products(g, zs)

    for d in hops[1:]:
        send_wd(d)

    rn = iota((rows, rows), 0)
    src = ((rn // (2 * nz * n)) * nz + (rn % (2 * nz)) // 2) * g2 + ((rn // (2 * nz)) % n) * 2 + rn % 2
    order = onehot(iota((rows, rows), 1) == src)
    raised = part_ref[g]
    for d in hops:
        for dz in range(nz):
            arrived(partin_ref.at[d - 1, :, add(zl, nz - dz, nz)], pt_r.at[dz, d])
        raised = raised + partin_ref[d - 1]
    raised = raised.reshape(rows, 128)
    hidden = (raised / (1.0 + jnp.exp(-raised))).astype(BF)

    hidden = dot(order, hidden).astype(BF)

    def hpiece(o_, z_):
        return hg_ref.at[o_, :, pl.ds(pl.multiple_of(z_ * 128, 128), 128)]

    hg_ref[o, :, pl.ds(pl.multiple_of(zl * 128, 128), 128)] = hidden
    own = hpiece(o, zl)
    for d in range(1, nz):
        send(own, own, hz_s.at[d], hz_r.at[d], dev(req, add(zl, d, nz), ex))
    spread(own, at_other, ho_s.at[0], ho_r.at[0])
    acc_ref[...] = jnp.zeros_like(acc_ref)
    for dz in range(1, nz):
        piece = hpiece(o, add(zl, nz - dz, nz))
        arrived(piece, hz_r.at[dz])
        spread(piece, at_other, ho_s.at[dz], ho_r.at[dz])

    unit_of = iota((1, nz * 128), 1) % 128
    masks = [onehot(jnp.logical_and(unit_of >= k * fs, unit_of < (k + 1) * fs)) for k in range(3)]

    def lower(o_):
        h = hg_ref[o_]
        w = wd_ref[pl.ds(pl.multiple_of(o_ * (nz * 128), 128), nz * 128), :]
        for k in range(3):
            acc_ref[k] += dot(h * masks[k], w)

    keep_wd.wait()
    for d in hops:
        arrived(wd_part(add(g, n - d)), wd_r.at[d])
    lower(o)
    for d in (1, 3, 2) if n == 4 else hops:
        os = add(o, n - d)
        for dz in range(nz):
            arrived(hpiece(os, add(zl, nz - dz, nz)), ho_r.at[dz, d])
        lower(os)

    rz = 2 * nz
    for k in range(3):
        r1s_ref[:, k] = acc_ref[k].reshape(plane, rz, n * 128).astype(BF)
    spot = o * n + g

    def r1_send(d, carry):
        i = add(spot, d, plane)
        remote(
            r1s_ref.at[i], r1r_ref.at[req], r1_s.at[0], r1_r.at[o],
            dev(rid(i % n, i // n, c), zl, ex),
        ).start()
        return carry

    lax.fori_loop(1, plane, r1_send, 0)
    keep = pltpu.make_async_copy(r1s_ref.at[spot], r1r_ref.at[req], loc_sem.at[6])
    keep.start()

    ro = iota((nz * 8, 32), 0)
    low = ro % 8
    order = onehot(jnp.logical_and(
        iota((nz * 8, 32), 1) == (low // 2) * rz + (ro // 8) * 2 + low % 2, low < 6))

    rw = iota((g2 * mr, 128), 0)
    low = rw % 8
    expert = jnp.where(low < 6, (rw // mr) * 3 + low // 2 + 1, -1)
    padded = ids_pad[...].astype(I32)
    weights = wt_ref[...]
    ids_pad[0:3, 0:toks] = weights
    weights = ids_pad[...]
    named = jnp.zeros((g2 * mr, 128), F32)
    weight = jnp.zeros((g2 * mr, 128), F32)
    for kk in range(3):
        hit = padded[kk:kk + 1, :] == expert
        named = named + jnp.where(hit, 1.0, 0.0)
        weight = weight + jnp.where(hit, weights[kk:kk + 1, :], 0.0)
    before = dot(named.astype(BF), onehot(r128 < c128))
    comb = jnp.where(before == (rw % 2).astype(F32), weight, 0.0)
    both = [jnp.where((rw % mr) // 8 == i, comb, 0.0).T[0:16] for i in range(hn)]
    both = jnp.concatenate(both, axis=0)
    p0 = both.astype(BF).astype(F32)
    p1 = (both - p0).astype(BF).astype(F32)
    parts = jnp.concatenate([p0, p1, both - p0 - p1], axis=0).astype(BF)

    spot2 = zl * g2 + ex
    keep.wait()
    mate = o + 1 - 2 * (o % 2)
    pairs = [(o, mate)] + ([(add(o, 2), add(mate, 2))] if n == 4 else [])
    for at, pair in enumerate(pairs):
        for here, os in enumerate(pair):
            own = at == 0 and here == 0
            arrived(r1s_ref.at[pl.ds(0, n - 1 if own else n)], r1_r.at[os])
            whole = r1r_ref[rid(0, os, c)].astype(F32)
            for gs in range(1, n):
                whole = whole + r1r_ref[rid(gs, os, c)].astype(F32)
            whole = whole.reshape(3 * rz, n * 128)
            whole = jnp.concatenate([whole, jnp.zeros((32 - 3 * rz, n * 128), F32)], axis=0)
            whole = dot(order, whole.astype(BF))
            for gd in range(n):
                r2s_ref[:, rid(gd, os, c)] = whole[:, gd * 128:(gd + 1) * 128].reshape(nz, 8, 128).astype(BF)

        def r2_send(i, carry):
            zt, rest = i // n, i % n
            y2 = (pair[0] // 2 * 2 + rest // hn) * (1 - c) + rest * c
            x2 = (rest % hn) * (1 - c) + (pair[0] // 2) * c
            e2 = y2 * 2 + x2
            src = r2s_ref.at[zt, pl.ds(y2 * n + x2 * hn, hn)]
            mine = zt * g2 + e2 == spot2

            @pl.when(mine)
            def _():
                pltpu.make_async_copy(src, r2r_ref.at[spot2], r2_r.at[0]).start()

            @pl.when(jnp.logical_not(mine))
            def _():
                remote(src, r2r_ref.at[spot2], r2_s.at[0], r2_r.at[0], dev(req, zt, e2)).start()

            return carry

        lax.fori_loop(0, n * nz, r2_send, 0)
    arrived(r2r_ref, r2_r.at[0])

    sums = [dot(parts, r2r_ref[z * g2:(z + 1) * g2].astype(F32).reshape(g2 * mr, 128).astype(BF)) for z in range(nz)]
    sums = jnp.concatenate(sums, axis=1)
    sums = sums[0:16 * hn] + (sums[16 * hn:32 * hn] + sums[32 * hn:48 * hn])
    pieces = []
    for i in range(hn):
        for z in range(nz):
            pieces.append(sums[i * 16:i * 16 + toks, z * 128:z * 128 + dn])
    total = jnp.concatenate(pieces, axis=1)
    out_ref[...] = (x_ref[...].astype(F32) + total).astype(BF)

    for cp in sends:
        cp.wait_send()

    @pl.when(jnp.logical_not(home))
    def _():
        first.wait_send()
    arrived(r1s_ref.at[pl.ds(0, plane - 1)], r1_s.at[0])
    arrived(r2r_ref.at[pl.ds(0, column - 1)], r2_s.at[0])


def shards(moe_input, route_ids, route_weight, w_up, w_down, queries, keys, values):
    nz = lax.axis_size("head")
    n = math.isqrt(lax.axis_size("req"))
    toks, width = moe_input.shape
    fs = w_up.shape[1]
    dn = w_down.shape[2]
    ffh = w_down.shape[1]
    heads, hd = queries.shape[1:]
    length = keys.shape[1]
    dq = 2 * width
    rows = 2 * n * n * nz
    plane = n * n
    vm = pl.BlockSpec(memory_space=pltpu.VMEM)
    hbm = pl.BlockSpec(memory_space=pl.ANY)
    dma = pltpu.SemaphoreType.DMA
    moe, ctx = pl.pallas_call(
        functools.partial(kernel, n, nz),
        out_shape=(
            jax.ShapeDtypeStruct((toks, width), BF),
            jax.ShapeDtypeStruct((heads, hd), BF),
        ),
        in_specs=[vm, vm, hbm, hbm, hbm, hbm, hbm, hbm],
        out_specs=(vm, vm),
        scratch_shapes=[
            pltpu.VMEM((toks, width), BF),
            pltpu.VMEM((heads, hd), BF),
            pltpu.VMEM((length, hd), BF),
            pltpu.VMEM((length, hd), BF),
            pltpu.VMEM((3, dn, ffh), BF),
            pltpu.VMEM((n, 3, fs, dq), BF),
            pltpu.VMEM((n, 256, width), BF),
            pltpu.VMEM((n, n * nz * 128, 128), BF),
            pltpu.VMEM((n * nz * 128, n * 128), BF),
            pltpu.VMEM((128, 128), BF),
            pltpu.VMEM((128, 128), F32),
            pltpu.VMEM((96 * n, 128), BF),
            pltpu.VMEM((96 * n, 128), BF),
            pltpu.VMEM((n, nz, 12 * n, width), BF),
            pltpu.VMEM((n, n, nz, 2 * n, 128), F32),
            pltpu.VMEM((n - 1, n, nz, 2 * n, 128), F32),
            pltpu.VMEM((n, rows, nz * 128), BF),
            pltpu.VMEM((3, rows, n * 128), F32),
            pltpu.VMEM((plane, 3, 2 * nz, n * 128), BF),
            pltpu.VMEM((plane, 3, 2 * nz, n * 128), BF),
            pltpu.VMEM((nz, plane, 8, 128), BF),
            pltpu.VMEM((2 * n * nz, n // 2, 8, 128), BF),
            dma((9,)),
            dma((n,)), dma((n,)),
            dma((2 * n,)), dma((2 * n,)),
            dma((nz,)), dma((nz,)),
            dma((nz, n)), dma((nz, n)),
            dma((nz, n)), dma((nz, n)),
            dma((n,)), dma((n,)),
            dma((nz,)), dma((nz,)),
            dma((nz, n)), dma((nz, n)),
            dma((1,)), dma((n,)),
            dma((1,)), dma((1,)),
        ],
        compiler_params=pltpu.CompilerParams(
            collective_id=0, has_side_effects=True, vmem_limit_bytes=55 * 1024 * 1024
        ),
        cost_estimate=pl.CostEstimate(flops=10**9, bytes_accessed=10**7, transcendentals=10**5),
        name="decode",
    )(
        route_ids.T, route_weight.T, moe_input, queries[0], keys[0], values[0], w_up,
        jnp.swapaxes(w_down, 1, 2),
    )
    return (moe, ctx[None])


def solution(mesh):
    placed = (
        P(("req", "head"), "exp"),
        P(("req", "head"), None),
        P(("req", "head"), None),
        P("exp", ("req", "head"), None),
        P("exp", None, ("req", "head")),
        P(("req", "head", "exp"), None, None),
        P(("req", "head", "exp"), None, None),
        P(("req", "head", "exp"), None, None),
    )
    return jax.shard_map(
        shards,
        mesh=mesh,
        in_specs=placed,
        out_specs=(P(("req", "head"), "exp"), P(("req", "head", "exp"), None, None)),
        check_vma=False,
    )
```

```python
import functools
import math

import jax
import jax.numpy as jnp
from jax import lax
from jax.experimental import pallas as pl
from jax.experimental.pallas import tpu as pltpu
from jax.sharding import PartitionSpec as P

BF = jnp.bfloat16
F32 = jnp.float32
I32 = jnp.int32
NT = (((1,), (1,)), ((), ()))


def iota(shape, dim):
    return lax.broadcasted_iota(I32, shape, dim)


def onehot(match):
    return jnp.where(match, 1.0, 0.0).astype(BF)


def dot(a, b):
    return jnp.dot(a, b, preferred_element_type=F32)


def attend(q, k, v):
    scores = lax.dot_general(q, k, NT, preferred_element_type=F32) * (1.0 / math.sqrt(q.shape[1]))
    weights = jnp.exp(scores - jnp.max(scores, axis=1, keepdims=True))
    total = jnp.sum(weights, axis=1, keepdims=True)
    return (dot(weights.astype(BF), v) / total).astype(BF)


def kernel(
    n, nz,
    ids_ref, wt_ref, x_hbm, q_hbm, k_hbm, v_hbm, up_hbm, down_hbm,
    out_ref, ctx_ref,
    x_ref, q_ref, k_ref, v_ref, down_ref, up_ref, upcat_ref, wt_own, wd_ref,
    tok_ref, ids_pad, send1_ref, recv1_ref, xg_ref, part_ref, partin_ref,
    hg_ref, acc_ref, r1s_ref, r1r_ref, r2s_ref, r2r_ref,
    loc_sem, up_s, up_r, s1_s, s1_r, s2_s, s2_r, s3_s, s3_r,
    pt_s, pt_r, wd_s, wd_r, hz_s, hz_r, ho_s, ho_r,
    r1_s, r1_r, r2_s, r2_r,
):
    toks, width = x_ref.shape
    dq = 2 * width
    chunks = width // 128
    fs = up_ref.shape[2]
    dn = down_ref.shape[1]
    g2 = 2 * n
    unit = 12 * n
    rows = 2 * n * n * nz
    plane = n * n
    column = g2 * nz
    srcs = plane * nz
    hops = (2, 1, 3) if n == 4 else (1,)

    req, zl, ex = lax.axis_index("req"), lax.axis_index("head"), lax.axis_index("exp")
    y, x = req // n, req % n
    zh, c = ex // 2, ex % 2
    g = x * (1 - c) + y * c
    o = y * (1 - c) + x * c

    def rid(g_, o_, c_):
        return (o_ * (1 - c_) + g_ * c_) * n + g_ * (1 - c_) + o_ * c_

    def dev(r_, zl_, ex_):
        return {"req": r_, "head": zl_, "exp": ex_}

    def turned(z, f):
        return z + f * (1 - 2 * (z % 2)) if nz > 1 else z

    def remote(src, dst, ss, rs, where):
        return pltpu.make_async_remote_copy(
            src_ref=src, dst_ref=dst, send_sem=ss, recv_sem=rs,
            device_id=where, device_id_type=pl.DeviceIdType.MESH,
        )

    def arrived(ref, sem):
        pltpu.make_async_copy(ref, ref, sem).wait()

    def add(v, d, m=n):
        return (v + d) % m

    away = (zh - g + n) % n
    odd = (away // 2) * (1 - away % 2) if n == 4 else away

    sends = []

    def send(src, dst, ss, rs, where):
        cp = remote(src, dst, ss, rs, where)
        cp.start()
        sends.append(cp)

    def at_group(d):
        return dev(rid(add(g, d), o, c), zl, ex)

    def at_other(d):
        return dev(rid(g, add(o, d), c), zl, ex)

    def spread(block, where, ss, rs):
        for d in hops:
            send(block, block, ss.at[d], rs.at[d], where(d))

    loads = [
        (x_hbm, x_ref), (q_hbm, q_ref), (k_hbm, k_ref), (v_hbm, v_ref),
        (up_hbm.at[:, :, pl.ds(g * dq, dq)], up_ref.at[g]), (down_hbm, down_ref),
    ]
    loads = [pltpu.make_async_copy(a, b, loc_sem.at[i]) for i, (a, b) in enumerate(loads)]
    for cp in loads:
        cp.start()
    load_x, load_q, load_k, load_v, load_up, load_down = loads

    barrier = pltpu.get_barrier_semaphore()

    def greet(where):
        pl.semaphore_signal(barrier, inc=1, device_id=where, device_id_type=pl.DeviceIdType.MESH)

    def greet_plane(d, carry):
        greet(dev(add(req, d, plane), zl, ex))
        return carry

    def greet_column(d, carry):
        m = add(zl * g2 + ex, d, column)
        greet(dev(req, m // g2, m % g2))
        return carry

    targets = []
    for dz in hops + (0,):
        for dt in range(2):
            t = (c + dt) % 2
            g_t = x * (1 - t) + y * t
            o_t = y * (1 - t) + x * t
            zt = add(zh, dz)
            targets.append((t, g_t, zt, dev(rid(zh, o_t, t), turned(zl, 1 if dz == n // 2 else 0), zt * 2 + t), dt == 0 and dz == 0))
    home = g == zh
    for t, g_t, zt, where, own in targets:
        if own:
            @pl.when(jnp.logical_not(home))
            def _():
                greet(where)
        else:
            greet(where)
    for dt in range(2):
        cs = (c + dt) % 2
        for dg in range(n):
            gs = add(g, dg)
            where = dev(rid(gs, o, c), turned(zl, odd), g * 2 + cs)
            if dt == 0 and dg == 0:
                @pl.when(jnp.logical_not(home))
                def _():
                    greet(where)
            else:
                greet(where)

    lax.fori_loop(1, column, greet_column, 0)
    lax.fori_loop(1, plane, greet_plane, 0)

    ids_pad[...] = jnp.zeros_like(ids_pad)
    ids_pad[0:3, 0:toks] = (ids_ref[...] + 1).astype(F32)
    hn = n // 2
    mr = hn * 8
    r128, c128 = iota((128, 128), 0), iota((128, 128), 1)
    tile = onehot(jnp.logical_and(c128 % 16 == r128, r128 < 16))
    tiled = dot(ids_pad[...].astype(BF), tile).astype(I32)
    tri = onehot(jnp.logical_and(r128 // 16 == c128 // 16, r128 % 16 < c128 % 16))
    grp = lax.broadcasted_iota(I32, (g2, 48, 128), 0)
    sub = lax.broadcasted_iota(I32, (g2, 48, 128), 1)
    lane = lax.broadcasted_iota(I32, (g2, 48, 128), 2)
    here = (lane // 16 == sub % 8).reshape(g2 * 48, 128)
    expert = (grp * 3 + sub // 16 + 1).reshape(g2 * 48, 128)
    slot = ((sub // 8) % 2).astype(F32).reshape(g2 * 48, 128)
    named = jnp.zeros((g2 * 48, 128), F32)
    for kk in range(3):
        hit = jnp.logical_and(here, tiled[kk:kk + 1, :] == expert)
        named = named + jnp.where(hit, 1.0, 0.0)
    before = dot(named.astype(BF), tri)
    pick = jnp.where(before == slot, named, 0.0).astype(BF)
    tok_ref[...] = jnp.zeros_like(tok_ref)
    load_x.wait()
    for ch in range(chunks):
        tok_ref[ch * 16:ch * 16 + toks, :] = x_ref[:, ch * 128:(ch + 1) * 128]
    send1_ref[...] = dot(pick, tok_ref[...]).astype(BF)

    @pl.when(home)
    def _():
        pl.semaphore_wait(barrier, plane - 1 + column - 1 + 2 * (2 * n - 1))

    @pl.when(jnp.logical_not(home))
    def _():
        pl.semaphore_wait(barrier, plane - 1 + column - 1 + 2 * (2 * n))

    first = None
    for at, (t, g_t, zt, where, own) in enumerate(targets):
        src = send1_ref.at[pl.ds((zt * 2 + t) * 48, 48), :]
        place = c * n + g_t
        dst = recv1_ref.at[pl.ds(place * 48, 48), :]
        cp = remote(src, dst, s1_s.at[at], s1_r.at[place], where)
        if own:
            first = cp

            @pl.when(home)
            def _():
                pltpu.make_async_copy(src, dst, s1_r.at[place]).start()

            @pl.when(jnp.logical_not(home))
            def _():
                cp.start()
        else:
            cp.start()
            sends.append(cp)

    for d in hops:
        send(
            up_hbm.at[:, :, pl.ds(add(g, d) * dq, dq)], up_ref.at[g],
            up_s.at[d], up_r.at[d], at_group(d),
        )

    load_q.wait()
    load_k.wait()
    load_v.wait()
    ctx_ref[...] = attend(q_ref[...], k_ref[...], v_ref[...])

    batch = min(16, srcs)

    def spread_down(i):
        t = [down_ref[k, :, i * batch * fs:(i + 1) * batch * fs].astype(F32).T for k in range(3)]
        for s in range(batch):
            parts = [t[k][s * fs:(s + 1) * fs] for k in range(3)]
            parts.append(jnp.zeros((128 - 3 * fs, dn), F32))
            at = i * batch + s
            xs, ys = (at // nz) % n, at // nz // n
            gs, os = xs * (1 - c) + ys * c, ys * (1 - c) + xs * c
            row = pl.multiple_of((os * nz + at % nz) * 128, 128)
            wt_own[gs, pl.ds(row, 128), 0:dn] = jnp.concatenate(parts, axis=0).astype(BF)

    load_down.wait()
    wt_own[...] = jnp.zeros_like(wt_own)
    for i in range(srcs // batch):
        spread_down(i)

    def wd_part(g_):
        return wd_ref.at[:, pl.ds(pl.multiple_of(g_ * 128, 128), 128)]

    def send_wd(d):
        send(wt_own.at[add(g, d)], wd_part(g), wd_s.at[d], wd_r.at[d], at_group(d))

    send_wd(hops[0])
    keep_wd = pltpu.make_async_copy(wt_own.at[g], wd_part(g), loc_sem.at[8])
    keep_wd.start()

    ru = lax.broadcasted_iota(I32, (chunks, unit, g2 * 48), 1)
    ch = lax.broadcasted_iota(I32, (chunks, unit, g2 * 48), 0)
    col = lax.broadcasted_iota(I32, (chunks, unit, g2 * 48), 2)
    second = jnp.where(ru >= 6 * n, 1, 0)
    rest = ru - 6 * n * second
    origin = (second * n + (rest % g2) // 2) * 48 + (rest // g2) * 16 + (rest % 2) * 8 + ch
    order = onehot(col == origin).reshape(chunks * unit, g2 * 48)
    for i in range(g2):
        arrived(recv1_ref.at[pl.ds(i * 48, 48), :], s1_r.at[i])
    placed = dot(order, recv1_ref[...]).astype(BF)
    for ch in range(chunks):
        xg_ref[o, turned(zl, odd), :, ch * 128:(ch + 1) * 128] = placed[ch * unit:(ch + 1) * unit]

    own = xg_ref.at[o, turned(zl, odd)]
    for d in range(1, nz):
        send(own, own, s2_s.at[d], s2_r.at[d], dev(req, add(zl, d, nz), ex))

    def x_from(dz):
        return lambda d: xg_ref.at[add(o, d), turned(add(zl, nz - dz, nz), odd)]

    spread(own, at_other, s3_s.at[0], s3_r.at[0])
    for dz in range(1, nz):
        block = x_from(dz)(0)
        arrived(block, s2_r.at[dz])
        spread(block, at_other, s3_s.at[dz], s3_r.at[dz])

    def fix_up(p):
        for h in range(2):
            parts = [up_ref[p, k, :, h * width:(h + 1) * width].astype(F32) for k in range(3)]
            parts.append(jnp.zeros((128 - 3 * fs, width), F32))
            upcat_ref[p, h * 128:(h + 1) * 128, :] = jnp.concatenate(parts, axis=0).astype(BF)

    load_up.wait()
    fix_up(g)
    for d in hops:
        p = add(g, n - d)
        arrived(up_ref.at[p], up_r.at[d])
        fix_up(p)

    band = iota((1, 1, 128), 2)

    def products(p, zs):
        a = xg_ref[:, zs].reshape(n * unit, width)
        r = lax.dot_general(a, upcat_ref[p], NT, preferred_element_type=F32)
        r = r.reshape(n, unit, 256)
        total = jnp.zeros((n, g2, 128), F32)
        for h in range(2):
            rk = [
                r[:, (3 * h + k) * g2:(3 * h + k + 1) * g2, h * 128:(h + 1) * 128]
                for k in range(3)
            ]
            total = total + jnp.where(band < fs, rk[0], jnp.where(band < 2 * fs, rk[1], rk[2]))
        part_ref[p, :, zs] = total

    for dz in range(nz):
        for d in hops:
            arrived(x_from(dz)(n - d), s3_r.at[dz, d])
        zs = turned(add(zl, nz - dz, nz), odd)
        for d in hops:
            p = add(g, d)
            products(p, zs)
            send(
                part_ref.at[p, :, zs], partin_ref.at[d - 1, :, zs],
                pt_s.at[dz, d], pt_r.at[dz, d], at_group(d),
            )
        products(g, zs)

    for d in hops[1:]:
        send_wd(d)

    rn = iota((rows, rows), 0)
    src = ((rn // (2 * nz * n)) * nz + (rn % (2 * nz)) // 2) * g2 + ((rn // (2 * nz)) % n) * 2 + rn % 2
    order = onehot(iota((rows, rows), 1) == src)
    raised = part_ref[g]
    for d in hops:
        for dz in range(nz):
            arrived(partin_ref.at[d - 1, :, add(zl, nz - dz, nz)], pt_r.at[dz, d])
        raised = raised + partin_ref[d - 1]
    raised = raised.reshape(rows, 128)
    hidden = (raised / (1.0 + jnp.exp(-raised))).astype(BF)

    hidden = dot(order, hidden).astype(BF)

    def hpiece(o_, z_):
        return hg_ref.at[o_, :, pl.ds(pl.multiple_of(z_ * 128, 128), 128)]

    hg_ref[o, :, pl.ds(pl.multiple_of(zl * 128, 128), 128)] = hidden
    own = hpiece(o, zl)
    for d in range(1, nz):
        send(own, own, hz_s.at[d], hz_r.at[d], dev(req, add(zl, d, nz), ex))
    spread(own, at_other, ho_s.at[0], ho_r.at[0])
    acc_ref[...] = jnp.zeros_like(acc_ref)
    for dz in range(1, nz):
        piece = hpiece(o, add(zl, nz - dz, nz))
        arrived(piece, hz_r.at[dz])
        spread(piece, at_other, ho_s.at[dz], ho_r.at[dz])

    unit_of = iota((1, nz * 128), 1) % 128
    masks = [onehot(jnp.logical_and(unit_of >= k * fs, unit_of < (k + 1) * fs)) for k in range(3)]

    def lower(o_):
        h = hg_ref[o_]
        w = wd_ref[pl.ds(pl.multiple_of(o_ * (nz * 128), 128), nz * 128), :]
        for k in range(3):
            acc_ref[k] += dot(h * masks[k], w)

    keep_wd.wait()
    for d in hops:
        arrived(wd_part(add(g, n - d)), wd_r.at[d])
    lower(o)
    for d in (1, 3, 2) if n == 4 else hops:
        os = add(o, n - d)
        for dz in range(nz):
            arrived(hpiece(os, add(zl, nz - dz, nz)), ho_r.at[dz, d])
        lower(os)

    rz = 2 * nz
    for k in range(3):
        r1s_ref[:, k] = acc_ref[k].reshape(plane, rz, n * 128).astype(BF)
    spot = o * n + g

    mate = o + 1 - 2 * (o % 2)
    pairs = [(o, mate)] + ([(add(o, 2), add(mate, 2))] if n == 4 else [])
    for at, os in enumerate(os for pair in pairs for os in pair):
        for dg in range(0 if at else 1, n):
            gs = add(g, dg)
            remote(
                r1s_ref.at[os * n + gs], r1r_ref.at[req], r1_s.at[0], r1_r.at[o],
                dev(rid(gs, os, c), zl, ex),
            ).start()
    keep = pltpu.make_async_copy(r1s_ref.at[spot], r1r_ref.at[req], loc_sem.at[6])
    keep.start()

    ro = iota((nz * 8, 32), 0)
    low = ro % 8
    order = onehot(jnp.logical_and(
        iota((nz * 8, 32), 1) == (low // 2) * rz + (ro // 8) * 2 + low % 2, low < 6))

    rw = iota((g2 * mr, 128), 0)
    low = rw % 8
    expert = jnp.where(low < 6, (rw // mr) * 3 + low // 2 + 1, -1)
    padded = ids_pad[...].astype(I32)
    weights = wt_ref[...]
    ids_pad[0:3, 0:toks] = weights
    weights = ids_pad[...]
    named = jnp.zeros((g2 * mr, 128), F32)
    weight = jnp.zeros((g2 * mr, 128), F32)
    for kk in range(3):
        hit = padded[kk:kk + 1, :] == expert
        named = named + jnp.where(hit, 1.0, 0.0)
        weight = weight + jnp.where(hit, weights[kk:kk + 1, :], 0.0)
    before = dot(named.astype(BF), onehot(r128 < c128))
    comb = jnp.where(before == (rw % 2).astype(F32), weight, 0.0)
    both = [jnp.where((rw % mr) // 8 == i, comb, 0.0).T[0:16] for i in range(hn)]
    both = jnp.concatenate(both, axis=0)
    p0 = both.astype(BF).astype(F32)
    p1 = (both - p0).astype(BF).astype(F32)
    parts = jnp.concatenate([p0, p1, both - p0 - p1], axis=0).astype(BF)

    spot2 = zl * g2 + ex
    keep.wait()
    for at, pair in enumerate(pairs):
        for here, os in enumerate(pair):
            own = at == 0 and here == 0
            arrived(r1s_ref.at[pl.ds(0, n - 1 if own else n)], r1_r.at[os])
            whole = r1r_ref[rid(0, os, c)].astype(F32)
            for gs in range(1, n):
                whole = whole + r1r_ref[rid(gs, os, c)].astype(F32)
            whole = whole.reshape(3 * rz, n * 128)
            whole = jnp.concatenate([whole, jnp.zeros((32 - 3 * rz, n * 128), F32)], axis=0)
            whole = dot(order, whole.astype(BF))
            for gd in range(n):
                r2s_ref[:, rid(gd, os, c)] = whole[:, gd * 128:(gd + 1) * 128].reshape(nz, 8, 128).astype(BF)

        def r2_send(i, carry):
            zt, rest = i // n, i % n
            y2 = (pair[0] // 2 * 2 + rest // hn) * (1 - c) + rest * c
            x2 = (rest % hn) * (1 - c) + (pair[0] // 2) * c
            e2 = y2 * 2 + x2
            src = r2s_ref.at[zt, pl.ds(y2 * n + x2 * hn, hn)]
            mine = zt * g2 + e2 == spot2

            @pl.when(mine)
            def _():
                pltpu.make_async_copy(src, r2r_ref.at[spot2], r2_r.at[0]).start()

            @pl.when(jnp.logical_not(mine))
            def _():
                remote(src, r2r_ref.at[spot2], r2_s.at[0], r2_r.at[0], dev(req, zt, e2)).start()

            return carry

        lax.fori_loop(0, n * nz, r2_send, 0)
    for cp in sends:
        cp.wait_send()

    @pl.when(jnp.logical_not(home))
    def _():
        first.wait_send()
    arrived(r1s_ref.at[pl.ds(0, plane - 1)], r1_s.at[0])
    arrived(r2r_ref.at[pl.ds(0, column - 1)], r2_s.at[0])

    arrived(r2r_ref, r2_r.at[0])

    sums = [dot(parts, r2r_ref[z * g2:(z + 1) * g2].astype(F32).reshape(g2 * mr, 128).astype(BF)) for z in range(nz)]
    sums = jnp.concatenate(sums, axis=1)
    sums = sums[0:16 * hn] + (sums[16 * hn:32 * hn] + sums[32 * hn:48 * hn])
    pieces = []
    for i in range(hn):
        for z in range(nz):
            pieces.append(sums[i * 16:i * 16 + toks, z * 128:z * 128 + dn])
    total = jnp.concatenate(pieces, axis=1)
    out_ref[...] = (x_ref[...].astype(F32) + total).astype(BF)


def shards(moe_input, route_ids, route_weight, w_up, w_down, queries, keys, values):
    nz = lax.axis_size("head")
    n = math.isqrt(lax.axis_size("req"))
    toks, width = moe_input.shape
    fs = w_up.shape[1]
    dn = w_down.shape[2]
    ffh = w_down.shape[1]
    heads, hd = queries.shape[1:]
    length = keys.shape[1]
    dq = 2 * width
    rows = 2 * n * n * nz
    plane = n * n
    vm = pl.BlockSpec(memory_space=pltpu.VMEM)
    hbm = pl.BlockSpec(memory_space=pl.ANY)
    dma = pltpu.SemaphoreType.DMA
    moe, ctx = pl.pallas_call(
        functools.partial(kernel, n, nz),
        out_shape=(
            jax.ShapeDtypeStruct((toks, width), BF),
            jax.ShapeDtypeStruct((heads, hd), BF),
        ),
        in_specs=[vm, vm, hbm, hbm, hbm, hbm, hbm, hbm],
        out_specs=(vm, vm),
        scratch_shapes=[
            pltpu.VMEM((toks, width), BF),
            pltpu.VMEM((heads, hd), BF),
            pltpu.VMEM((length, hd), BF),
            pltpu.VMEM((length, hd), BF),
            pltpu.VMEM((3, dn, ffh), BF),
            pltpu.VMEM((n, 3, fs, dq), BF),
            pltpu.VMEM((n, 256, width), BF),
            pltpu.VMEM((n, n * nz * 128, 128), BF),
            pltpu.VMEM((n * nz * 128, n * 128), BF),
            pltpu.VMEM((128, 128), BF),
            pltpu.VMEM((128, 128), F32),
            pltpu.VMEM((96 * n, 128), BF),
            pltpu.VMEM((96 * n, 128), BF),
            pltpu.VMEM((n, nz, 12 * n, width), BF),
            pltpu.VMEM((n, n, nz, 2 * n, 128), F32),
            pltpu.VMEM((n - 1, n, nz, 2 * n, 128), F32),
            pltpu.VMEM((n, rows, nz * 128), BF),
            pltpu.VMEM((3, rows, n * 128), F32),
            pltpu.VMEM((plane, 3, 2 * nz, n * 128), BF),
            pltpu.VMEM((plane, 3, 2 * nz, n * 128), BF),
            pltpu.VMEM((nz, plane, 8, 128), BF),
            pltpu.VMEM((2 * n * nz, n // 2, 8, 128), BF),
            dma((9,)),
            dma((n,)), dma((n,)),
            dma((2 * n,)), dma((2 * n,)),
            dma((nz,)), dma((nz,)),
            dma((nz, n)), dma((nz, n)),
            dma((nz, n)), dma((nz, n)),
            dma((n,)), dma((n,)),
            dma((nz,)), dma((nz,)),
            dma((nz, n)), dma((nz, n)),
            dma((1,)), dma((n,)),
            dma((1,)), dma((1,)),
        ],
        compiler_params=pltpu.CompilerParams(
            collective_id=0, has_side_effects=True, vmem_limit_bytes=55 * 1024 * 1024
        ),
        cost_estimate=pl.CostEstimate(flops=10**9, bytes_accessed=10**7, transcendentals=10**5),
        name="decode",
    )(
        route_ids.T, route_weight.T, moe_input, queries[0], keys[0], values[0], w_up,
        jnp.swapaxes(w_down, 1, 2),
    )
    return (moe, ctx[None])


def solution(mesh):
    placed = (
        P(("req", "head"), "exp"),
        P(("req", "head"), None),
        P(("req", "head"), None),
        P("exp", ("req", "head"), None),
        P("exp", None, ("req", "head")),
        P(("req", "head", "exp"), None, None),
        P(("req", "head", "exp"), None, None),
        P(("req", "head", "exp"), None, None),
    )
    return jax.shard_map(
        shards,
        mesh=mesh,
        in_specs=placed,
        out_specs=(P(("req", "head"), "exp"), P(("req", "head", "exp"), None, None)),
        check_vma=False,
    )
```
